128 devices in a mesh: head: 8 (over x, z_lo), ctx: 16 (over y, z_hi, core).
Axes of the slice: x: 4, y: 4, z: 4 (z_hi: 2, z_lo: 2; z = z_hi * 2 + z_lo), core: 2. Of those that a mesh axis runs over, the one named last changes fastest.
Arguments:
- query_states: bfloat16 [8, 16, 64, 4096], P(None, 'ctx', None, 'head'), may hold values from -8 to 8
- key_states: bfloat16 [8, 16, 64, 1024], P(None, 'ctx', None, 'head'), may hold values from -4 to 4
- value_states: bfloat16 [8, 16, 64, 1024], P(None, 'ctx', None, 'head'), may hold values from -6 to 6
- out_grad: bfloat16 [8, 16, 64, 4096], P(None, 'ctx', None, 'head'), may hold values from -6 to 6
- out_weight: bfloat16 [4096, 4096], P('head'), may hold values from -0.125 to 0.125
- vertical_blocks: int32 [8, 8, 16, 32], P('head', None, 'ctx'), may hold values from 0 to 127, as said below
- slash_offsets: int32 [8, 8, 16, 8], P('head', None, 'ctx'), may hold values from 0 to 15, as said below
Outputs:
- layer_out: bfloat16 [8, 16, 64, 4096], P(None, 'ctx', None, 'head')
- query_grad: bfloat16 [8, 16, 64, 4096], P(None, 'ctx', None, 'head')
- key_grad: bfloat16 [8, 16, 64, 1024], P(None, 'ctx', None, 'head')
- value_grad: bfloat16 [8, 16, 64, 1024], P(None, 'ctx', None, 'head')
The draws below stay inside these ranges and needn't reach their ends.
Inputs may be any that keep to these rules, and one draw needn't show every extreme that they name: `vertical_blocks`: entries of one vertical list are distinct; a kept vertical block never equals a kept slash block of the same list. `slash_offsets`: the first offset of every list is 0; the offsets of one list are distinct.
All inputs are finite; a program needn't handle non-finite values.
Results may differ from the reference program's by a relative error of at most 0.023.
Values may be sent and summed in bfloat16 or wider, within the bound.
A program may use at most 192 MiB of HBM per device.

```python
import math
import jax
import jax.numpy as jnp
from jax import lax

D = 4096
HQ = 32
KVH = 8
HD = 128
BLK = 64
NV = 32
NS = 8
SWIN = 16
QB_DEV = 8
NBLK = 128
N_HEAD = 8
N_CTX = 16


def choose_lists(key):
    block_col = jnp.arange(NBLK, dtype=jnp.int32)[None, :, None]
    offsets = jnp.arange(1, SWIN, dtype=jnp.int32)
    first_rand = jax.random.randint(jax.random.fold_in(key, 21), (KVH, NBLK, SWIN - 1), 0, 4096)
    first_score = first_rand * SWIN + offsets
    forced = (block_col == NBLK - 1) & (offsets == SWIN - 1)
    first_score = jnp.where(forced, -1, first_score)
    unused, picked = lax.top_k(-first_score, NS - 1)
    slash_rows = jnp.concatenate([jnp.zeros((KVH, NBLK, 1), jnp.int32), (picked + 1).astype(jnp.int32)], axis=2)
    slash_blocks = block_col - slash_rows
    candidate = jnp.arange(NBLK, dtype=jnp.int32)
    taken = jnp.any(slash_blocks[..., None] == candidate[None, None, None, :], axis=2)
    second_rand = jax.random.randint(jax.random.fold_in(key, 22), (KVH, NBLK, NBLK), 0, 4096)
    big_value = 4096 * NBLK
    second_score = second_rand * NBLK + candidate
    second_score = jnp.where(candidate == 0, -1, second_score)
    later = candidate[None, None, :] > block_col
    second_score = jnp.where(later, big_value + (NBLK - candidate), second_score)
    second_score = jnp.where(taken | (candidate[None, None, :] == block_col), 2 * big_value + candidate, second_score)
    unused_two, vertical = lax.top_k(-second_score, NV)
    ctx_count = NBLK // QB_DEV
    vertical = vertical.astype(jnp.int32).reshape(KVH, QB_DEV, ctx_count, NV)
    slash_rows = slash_rows.reshape(KVH, QB_DEV, ctx_count, NS)
    return (vertical, slash_rows)


def draw_vertical_blocks(key, part):
    vertical, slash_rows = choose_lists(key)
    return vertical


def draw_slash_offsets(key, part):
    vertical, slash_rows = choose_lists(key)
    return slash_rows


def draw_query_states(key, part):
    key = jax.random.fold_in(key, 1)
    full_shape = (QB_DEV, NBLK // QB_DEV, BLK, HQ * HD)
    return jnp.clip(jax.random.normal(key, full_shape, jnp.float32), -6.0, 6.0).astype(jnp.bfloat16)


def draw_key_states(key, part):
    key = jax.random.fold_in(key, 2)
    full_shape = (QB_DEV, NBLK // QB_DEV, BLK, KVH * HD)
    return jnp.clip(jax.random.normal(key, full_shape, jnp.float32), -4.0, 4.0).astype(jnp.bfloat16)


def raised(values, key, source, target, shards_of, factor):
    def block_of(axis_at):
        return (jnp.arange(values.shape[axis_at]) // (values.shape[axis_at] // shards_of)).reshape((-1,) + (1,) * (values.ndim - 1 - axis_at))

    first = jax.random.permutation(key, shards_of)[block_of(target)]
    other_side = (block_of(target) + shards_of // 2) % shards_of
    return jnp.where((block_of(source) == first) | (block_of(source) == other_side), factor * values, values)


def block_levels(key, shape, shards, low, high):
    factor_of, own = 1.0, jax.random.fold_in(key, 6)
    for axis_at, shards_of in shards:
        draws = jnp.exp(jax.random.uniform(jax.random.fold_in(own, axis_at), (shards_of,), jnp.float32, low / len(shards), high / len(shards)))
        factor_of = factor_of * jnp.repeat(draws, shape[axis_at] // shards_of).reshape([-1 if axis == axis_at else 1 for axis in range(len(shape))])
    return factor_of


def scatter_about(rng, extent, scale, bound, shards=(), kind=jnp.bfloat16):
    gain = block_levels(rng, extent, shards, -0.22, 0.18) if shards else 1.0
    values = jax.random.normal(rng, extent, jnp.float32) * scale * gain
    return jnp.minimum(jnp.maximum(values, -bound), bound).astype(kind)


def gaussian_with(rng, shape, width, limit, cuts, heavy, held_as=jnp.bfloat16):
    result = width * jax.random.normal(rng, shape, jnp.float32)
    if cuts:
        result = result * block_levels(rng, shape, cuts, -0.22, 0.18)
    return jnp.clip(raised(result, jax.random.fold_in(rng, 3), *heavy), -limit, limit).astype(held_as)


def setup_inputs(seed: int = 0) -> dict:
    keys = jax.random.split(jax.random.key(seed), 8)
    query_states = draw_query_states(jax.random.fold_in(keys[7], 71), 0)
    key_states = draw_key_states(jax.random.fold_in(keys[7], 71), 0)
    value_states = scatter_about(keys[2], (QB_DEV, N_CTX, BLK, KVH * HD), 1.0, 6.0, ((1, 16), (3, 8)))
    out_grad = scatter_about(keys[3], (QB_DEV, N_CTX, BLK, D), 1.0, 6.0, ((1, 16), (3, 8)))
    out_weight = gaussian_with(keys[4], (HQ * HD, D), (HQ * HD) ** -0.5, 0.125, ((0, 8),), (0, 1, 8, 2.0))
    vertical_blocks = draw_vertical_blocks(jax.random.fold_in(keys[7], 71), 0)
    slash_offsets = draw_slash_offsets(jax.random.fold_in(keys[7], 71), 0)
    return dict(query_states=query_states, key_states=key_states, value_states=value_states, out_grad=out_grad, out_weight=out_weight, vertical_blocks=vertical_blocks, slash_offsets=slash_offsets)


def entry_table(block_ids, vertical, slash_rows, nblk, block_rows):
    raw_index = jnp.concatenate([vertical, block_ids[:, None] - slash_rows], axis=1)
    is_kept = (raw_index >= 0) & (raw_index <= block_ids[:, None])
    on_diagonal = raw_index == block_ids[:, None]
    query_pos = lax.broadcasted_iota(jnp.int32, (block_rows, block_rows), 0)
    key_pos = lax.broadcasted_iota(jnp.int32, (block_rows, block_rows), 1)
    lower_tri = key_pos <= query_pos
    allowed = is_kept[:, None, :, None] & (jnp.logical_not(on_diagonal)[:, None, :, None] | lower_tri[None, :, None, :])
    return (jnp.clip(raw_index, 0, nblk - 1).astype(jnp.int32), allowed)

def attend_group(query_rows, key_rows, value_rows, grad_rows, allowed, score_scale):
    q32 = query_rows.astype(jnp.float32)
    k32 = key_rows.astype(jnp.float32)
    v32 = value_rows.astype(jnp.float32)
    g32 = grad_rows.astype(jnp.float32)
    scores = jnp.einsum('rqhd,rekd->rqhek', q32, k32) * score_scale
    scores = jnp.where(allowed[:, :, None], scores, -jnp.inf)
    row_max = lax.optimization_barrier(jnp.max(scores, axis=(3, 4), keepdims=True))
    expo = jnp.exp(scores - row_max)
    row_total = lax.optimization_barrier(jnp.sum(expo, axis=(3, 4), keepdims=True))
    log_norm = row_max + jnp.log(row_total)
    probs = (expo / row_total).astype(jnp.bfloat16)
    attended = jnp.einsum('rqhek,rekd->rqhd', probs.astype(jnp.float32), v32).astype(jnp.bfloat16)
    probs_back = jnp.exp(scores - log_norm)
    grad_probs = jnp.einsum('rqhd,rekd->rqhek', g32, v32)
    row_delta = lax.optimization_barrier(jnp.sum(g32 * attended.astype(jnp.float32), axis=-1))[:, :, :, None, None]
    grad_scores = (probs_back * (grad_probs - row_delta)).astype(jnp.bfloat16).astype(jnp.float32)
    probs_low = probs_back.astype(jnp.bfloat16).astype(jnp.float32)
    value_part = jnp.einsum('rqhek,rqhd->rekd', probs_low, g32)
    key_part = jnp.einsum('rqhek,rqhd->rekd', grad_scores, q32) * score_scale
    query_part = (jnp.einsum('rqhek,rekd->rqhd', grad_scores, k32) * score_scale).astype(jnp.bfloat16)
    return (attended, query_part, key_part, value_part)

def reference(query_states, key_states, value_states, out_grad, out_weight, vertical_blocks, slash_offsets):
    nblk = QB_DEV * N_CTX
    heads_per_kv = HQ // KVH
    score_scale = 1.0 / math.sqrt(HD)
    queries_all = query_states.reshape(nblk, BLK, HQ, HD)
    keys_all = key_states.reshape(nblk, BLK, KVH, HD)
    values_all = value_states.reshape(nblk, BLK, KVH, HD)
    grad_flat = out_grad.reshape(nblk * BLK, D)
    attn_grad = jnp.dot(grad_flat, out_weight.T, preferred_element_type=jnp.float32).astype(jnp.bfloat16)
    attn_grad = attn_grad.reshape(nblk, BLK, HQ, HD)
    per_step = math.gcd(nblk, 8)
    step_count = nblk // per_step
    vertical_all = vertical_blocks.reshape(KVH, step_count, per_step, NV)
    slash_all = slash_offsets.reshape(KVH, step_count, per_step, NS)
    block_ids = jnp.arange(nblk, dtype=jnp.int32).reshape(step_count, per_step)
    attended_list = []
    query_list = []
    partial_list = []
    for head_slot in range(KVH):
        first_head = head_slot * heads_per_kv
        q_part = queries_all[:, :, first_head:first_head + heads_per_kv].reshape(step_count, per_step, BLK, heads_per_kv, HD)
        g_part = attn_grad[:, :, first_head:first_head + heads_per_kv].reshape(step_count, per_step, BLK, heads_per_kv, HD)
        key_table = keys_all[:, :, head_slot]
        value_table = values_all[:, :, head_slot]

        def step_fn(running, inputs, key_table=key_table, value_table=value_table):
            q_rows, g_rows, ids_now, vertical, slash_rows = inputs
            key_index, allowed = entry_table(ids_now, vertical, slash_rows, nblk, BLK)
            attended, query_part, key_part, value_part = attend_group(q_rows, key_table[key_index], value_table[key_index], g_rows, allowed, score_scale)
            update = jnp.stack([key_part, value_part], axis=3).reshape(-1, BLK, 2, HD)
            running = running.at[key_index.reshape(-1)].add(update)
            return (running, (attended, query_part))
        initial = jnp.zeros((nblk, BLK, 2, HD), jnp.float32)
        partial_value, (attended_rows, query_rows) = lax.scan(step_fn, initial, (q_part, g_part, block_ids, vertical_all[head_slot], slash_all[head_slot]))
        attended_list.append(attended_rows.reshape(nblk, BLK, heads_per_kv * HD))
        query_list.append(query_rows.reshape(nblk, BLK, heads_per_kv * HD))
        partial_list.append(partial_value)
    attention = jnp.concatenate(attended_list, axis=2).reshape(nblk * BLK, HQ * HD)
    head_width = HQ * HD // N_HEAD
    layer_sum = jnp.zeros((nblk * BLK, D), jnp.float32)
    for shard_index in range(N_HEAD):
        partial_out = jnp.dot(attention[:, shard_index * head_width:(shard_index + 1) * head_width], out_weight[shard_index * head_width:(shard_index + 1) * head_width], preferred_element_type=jnp.float32).astype(jnp.bfloat16)
        partial_out = lax.optimization_barrier(partial_out)
        layer_sum = layer_sum + partial_out.astype(jnp.float32)
    layer_out = layer_sum.astype(jnp.bfloat16).reshape(out_grad.shape)
    query_grad = jnp.concatenate(query_list, axis=2).reshape(query_states.shape)
    stacked = jnp.stack(partial_list, axis=3)
    key_grad = stacked[:, :, 0].astype(jnp.bfloat16).reshape(key_states.shape)
    value_grad = stacked[:, :, 1].astype(jnp.bfloat16).reshape(value_states.shape)
    return (layer_out, query_grad, key_grad, value_grad)
```

```python
import functools
import math

import jax
import jax.numpy as jnp
from jax import lax
from jax.experimental import pallas as pl
from jax.experimental.pallas import tpu as pltpu
from jax.sharding import PartitionSpec as P

HD = 128
NG = 4
BLK = 64
ROWS = 8
NE = 40
EPC = 8
CK = EPC * BLK
NCH = NE // EPC
QN = NG * BLK
CHUNKS = 36
NOSLOT = CHUNKS * EPC
SCALE = 1.0 / math.sqrt(HD)
LOG2E = 1.4426950408889634
FAR = -1e30


def chunk_base(i):
    return jnp.where(i == 0, 0, jnp.where(i == 1, 2, 5 * i - 4))


def chunk_count(i):
    return jnp.minimum(NCH, 2 * (i + 1))


def lists(vertical, slash, me, n_ctx):
    rows = jnp.arange(ROWS, dtype=jnp.int32)
    bid = rows * n_ctx + me
    raw = jnp.concatenate([bid[:, None] - slash, vertical], axis=1)
    kept = (raw >= 0) & (raw <= bid[:, None])
    order = jnp.arange(NE, dtype=jnp.int32)
    place = jnp.sum((kept[:, None, :] & (order[None, None, :] < order[None, :, None])).astype(jnp.int32), axis=2)
    place = jnp.where(kept, place, NE)
    here = place[:, None, :] == order[None, :, None]
    moved = raw % n_ctx * ROWS + raw // n_ctx
    index = jnp.sum(jnp.where(here, moved[:, None, :], 0), axis=2)
    far = jnp.where(jnp.any(here, axis=2), 0.0, FAR).astype(jnp.float32)
    slot = chunk_base(rows)[:, None] * EPC + place
    block = jnp.arange(ROWS * n_ctx, dtype=jnp.int32)
    hit = (raw[:, None, :] == block[None, :, None]) & kept[:, None, :]
    where = NOSLOT + jnp.sum(jnp.where(hit, slot[:, None, :] - NOSLOT, 0), axis=2)
    return index, far, where


def dot(a, b, ca, cb):
    return lax.dot_general(a, b, (((ca,), (cb,)), ((), ())), preferred_element_type=jnp.float32)


def heads_down(x):
    return jnp.concatenate([x[:, h * HD:(h + 1) * HD] for h in range(NG)], axis=0)


def heads_across(x):
    return jnp.concatenate([x[h * BLK:(h + 1) * BLK] for h in range(NG)], axis=1)


def forward_row(i, index, far, q, kv, s):
    qs = heads_down(q[i])
    s.qs[i] = qs
    base, count = chunk_base(i), chunk_count(i)
    key_pos = lax.broadcasted_iota(jnp.int32, (BLK, QN), 0)
    query_pos = lax.broadcasted_iota(jnp.int32, (BLK, QN), 1) % BLK

    def scores(ch, top, first):
        for e in range(EPC):
            s.kvrow[ch, e * BLK:(e + 1) * BLK, :] = kv[index[i, ch * EPC + e]]
        sc = dot(s.kvrow[ch, :, :HD], qs, 1, 1)
        for e in range(EPC):
            part = sc[e * BLK:(e + 1) * BLK]
            if first and e == 0:
                part = jnp.where(key_pos <= query_pos, part, FAR)
            s.sc[ch, e * BLK:(e + 1) * BLK, :] = part
            part = jnp.max(part.reshape(BLK // 8, 8, QN), axis=0)
            top = jnp.maximum(top, part + far[i, ch * EPC + e])
        return top

    top = scores(0, jnp.full((8, QN), FAR, jnp.float32), True)
    top = lax.fori_loop(1, count, lambda ch, t: scores(ch, t, False), top)
    top = jnp.max(top, axis=0, keepdims=True) * (SCALE * LOG2E)

    def values(ch, carry):
        total, acc = carry
        for e in range(EPC):
            shift = top - far[i, ch * EPC + e]
            p = jnp.exp2(s.sc[ch, e * BLK:(e + 1) * BLK, :] * (SCALE * LOG2E) - shift)
            total = total + jnp.sum(p.reshape(BLK // 8, 8, QN), axis=0)
            s.p[base + ch, e * BLK:(e + 1) * BLK, :] = p.astype(jnp.bfloat16)
        acc = acc + dot(s.kvrow[ch, :, HD:], s.p[base + ch], 0, 0)
        return total, acc

    total, acc = lax.fori_loop(
        0, count, values, (jnp.zeros((8, QN), jnp.float32), jnp.zeros((HD, QN), jnp.float32))
    )
    inv = 1.0 / jnp.sum(total, axis=0, keepdims=True)
    out = (acc * inv).astype(jnp.bfloat16)
    s.ot[i] = out
    s.inv[i] = jnp.broadcast_to(inv, (8, QN))
    s.att[i] = heads_across(out.astype(jnp.float32).T.astype(jnp.bfloat16))


def backward_row(i, index, g, kv, s):
    base, count = chunk_base(i), chunk_count(i)
    gt = heads_down(g[i].astype(jnp.float32)).T
    gt = (gt * s.inv[i][0:1]).astype(jnp.bfloat16)
    g32 = gt.astype(jnp.float32)
    delta = jnp.sum(g32 * s.ot[i].astype(jnp.float32), axis=0, keepdims=True)
    s.gt[...] = gt
    s.gs[...] = g32.T.astype(jnp.bfloat16)

    def chunk(ch, acc):
        for e in range(EPC):
            s.kvrow[0, e * BLK:(e + 1) * BLK, :] = kv[index[i, ch * EPC + e]]
        dp = dot(s.kvrow[0, :, HD:], s.gt[...], 1, 0)
        p = s.p[base + ch]
        ds = (p.astype(jnp.float32) * (dp - delta)).astype(jnp.bfloat16)
        start = (base + ch) * EPC
        dk = dot(ds, s.qs[i], 1, 0)
        dv = dot(p, s.gs[...], 1, 0)
        s.slots[pl.ds(start, EPC), :, :HD] = dk.reshape(EPC, BLK, HD)
        s.slots[pl.ds(start, EPC), :, HD:] = dv.reshape(EPC, BLK, HD)
        return acc + dot(s.kvrow[0, :, :HD], ds, 0, 0)

    acc = lax.fori_loop(0, count, chunk, jnp.zeros((HD, QN), jnp.float32))
    s.dq[i] = heads_across((acc * SCALE).T).astype(jnp.bfloat16)


def collect(i, u, where, s):
    def more(r, acc):
        return acc + s.slots[where[r, u]]

    return lax.fori_loop(i, ROWS, more, jnp.zeros((BLK, 2 * HD), jnp.float32))


class Scratch:
    pass


MESH = pl.DeviceIdType.MESH
OG_PARTS = 4
OG_ROWS = ROWS // OG_PARTS
KV_PARTS = 2
KV_ROWS = ROWS // KV_PARTS


def send(src, dst, send_sem, recv_sem, device):
    pltpu.make_async_remote_copy(
        src_ref=src, dst_ref=dst, send_sem=send_sem, recv_sem=recv_sem, device_id=device, device_id_type=MESH
    ).start()


def sent(src, sem, device):
    pltpu.make_async_remote_copy(
        src_ref=src, dst_ref=src, send_sem=sem, recv_sem=sem, device_id=device, device_id_type=MESH
    ).wait_send()


def arrived(dst, sem, device):
    pltpu.make_async_remote_copy(
        src_ref=dst, dst_ref=dst, send_sem=sem, recv_sem=sem, device_id=device, device_id_type=MESH
    ).wait_recv()


class Place:
    def __init__(self):
        h, c = lax.axis_index("head"), lax.axis_index("ctx")
        self.h, self.c = h, c
        x, zl = h // 2, h % 2
        y, zh, core = c // 4, c // 2 % 2, c % 2
        self.y, self.zh, self.core = y, zh, core
        self.xp, self.xm, self.xo = [(x + k) % 4 * 2 + zl for k in (1, 3, 2)]
        self.zp = x * 2 + 1 - zl
        flip = 1 - 2 * zl
        self.xp_z, self.xm_z, self.xo_z = self.xp + flip, self.xm + flip, self.xo + flip
        self.ys = [(y + k) % 4 for k in (1, 3, 2)]
        self.yp, self.ym, self.yo = [v * 4 + zh * 2 + core for v in self.ys]
        turn = 2 * (1 - 2 * zh)
        self.zhp = c + turn
        self.yp_z, self.ym_z, self.yo_z = self.yp + turn, self.ym + turn, self.yo + turn
        self.other = 1 - 2 * core
        self.sib = c + self.other

    def on_head(self, index):
        return (index, self.c)

    def on_ctx(self, index):
        return (self.h, index)


def gather_out_grad(me, s):
    def piece(owner, k):
        return s.og.at[owner, pl.ds(k * OG_ROWS, OG_ROWS)]

    def go(kind, owner, to, k):
        ref = piece(owner, k)
        send(ref, ref, s.og_send.at[kind, k], s.og_recv.at[kind, k], me.on_head(to))

    def come(kind, owner, k):
        arrived(piece(owner, k), s.og_recv.at[kind, k], me.on_head(me.zp))

    def gone(kind, owner, k):
        sent(piece(owner, k), s.og_send.at[kind, k], me.on_head(me.zp))

    return go, come, gone


def gather_kv(me, s):
    def piece(owner, k):
        return s.kv.at[pl.ds(owner * ROWS + k * KV_ROWS, KV_ROWS)]

    def go(kind, owner, to, k):
        ref = piece(owner, k)
        send(ref, ref, s.kv_send.at[kind, k], s.kv_recv.at[kind, k], me.on_ctx(to))

    def come(kind, owner, k):
        arrived(piece(owner, k), s.kv_recv.at[kind, k], me.on_ctx(me.sib))

    def gone(kind, owner, k):
        sent(piece(owner, k), s.kv_send.at[kind, k], me.on_ctx(me.sib))

    return go, come, gone


def project_grad(owner, first, weight, s):
    cols = pl.ds(pl.multiple_of(owner * NG * HD, NG * HD), NG * HD)
    part = dot(s.og[owner].reshape(ROWS * BLK, NG * HD), weight[:, cols], 1, 1)
    for half in range(2):
        now = part[:, half * 2 * HD:(half + 1) * 2 * HD].reshape(ROWS, BLK, 2 * HD)
        at = slice(half * ROWS, (half + 1) * ROWS)
        s.slots[at] = now if first else s.slots[at] + now


def layer_kernel(n_ctx, index, far, where, q, key, value, out_grad, weight, layer_out, dq, dk, dv, *refs):
    s = Scratch()
    (
        s.qs, s.kvrow, s.sc, s.p, s.ot, s.inv, s.gt, s.gs, s.slots, s.att, s.g, s.kv, s.og,
        s.lo, s.s1, s.r1, s.s2, s.r2, s.s3, s.r3,
        s.og_send, s.og_recv, s.kv_send, s.kv_recv, s.lo_send, s.lo_recv,
        s.send1, s.recv1, s.send2, s.recv2, s.send3, s.recv3,
    ) = refs
    s.dq = dq
    me = Place()
    mine = pl.multiple_of(me.c * ROWS, ROWS)
    s.kv[pl.ds(mine, ROWS), :, :HD] = key[...]
    s.kv[pl.ds(mine, ROWS), :, HD:] = value[...]
    s.og[me.h] = out_grad[...]

    barrier = pltpu.get_barrier_semaphore()
    partners = [me.on_head(d) for d in (me.xp, me.xm, me.xo, me.zp)]
    partners += [me.on_ctx(d) for d in (me.zhp, me.yp, me.ym, me.yo, me.sib)]
    for device in partners:
        pl.semaphore_signal(barrier, inc=1, device_id=device, device_id_type=MESH)
    pl.semaphore_wait(barrier, len(partners))

    og_go, og_come, og_gone = gather_out_grad(me, s)
    kv_go, kv_come, kv_gone = gather_kv(me, s)
    kv_kinds = [
        (0, me.c, me.yp), (1, me.c, me.ym), (2, me.c, me.yo), (3, me.c, me.zhp),
        (4, me.zhp, me.yp), (5, me.zhp, me.ym), (6, me.zhp, me.yo),
        (7, me.c, me.sib), (8, me.zhp, me.sib), (9, me.ym, me.sib), (10, me.yp, me.sib), (11, me.yo, me.sib),
        (12, me.ym_z, me.sib), (13, me.yp_z, me.sib), (14, me.yo_z, me.sib),
    ]
    og_kinds = [
        (0, me.h, me.xp), (1, me.h, me.xm), (2, me.h, me.xo), (3, me.h, me.zp),
        (4, me.zp, me.xp), (5, me.zp, me.xm), (6, me.xo, me.zp),
    ]

    def kv_start(kinds, k):
        for kind in kinds:
            kv_go(*kv_kinds[kind], k)

    def og_start(kinds, k):
        for kind in kinds:
            og_go(*og_kinds[kind], k)

    @pl.loop(0, KV_PARTS)
    def _(k):
        kv_start((3, 0, 1, 2, 7), k)

    @pl.loop(0, OG_PARTS)
    def _(k):
        og_start((3,), k)

    @pl.loop(0, OG_PARTS)
    def _(k):
        og_start((0, 1, 2), k)

    s.slots[NOSLOT] = jnp.zeros((BLK, 2 * HD), jnp.float32)
    project_grad(me.h, True, weight, s)

    @pl.loop(0, KV_PARTS)
    def _(k):
        kv_come(3, me.zhp, k)
        kv_start((4, 5, 6, 8), k)

    @pl.loop(0, OG_PARTS)
    def _(k):
        og_come(3, me.zp, k)
        og_start((4, 5), k)

    project_grad(me.zp, False, weight, s)

    @pl.loop(0, KV_PARTS)
    def _(k):
        for kind, owner in ((0, me.ym), (1, me.yp), (2, me.yo)):
            kv_come(kind, owner, k)
            kv_start((kind + 9,), k)

    @pl.loop(0, OG_PARTS)
    def _(k):
        og_come(2, me.xo, k)
        og_start((6,), k)

    @pl.loop(0, KV_PARTS)
    def _(k):
        for kind, owner in ((4, me.ym_z), (5, me.yp_z), (6, me.yo_z)):
            kv_come(kind, owner, k)
            kv_start((kind + 8,), k)

    @pl.loop(0, KV_PARTS)
    def _(k):
        owners = (me.c, me.zhp, me.ym, me.yp, me.yo, me.ym_z, me.yp_z, me.yo_z)
        for kind, owner in enumerate(owners, 7):
            kv_come(kind, owner + me.other, k)

    project_grad(me.xo, False, weight, s)

    @pl.loop(0, ROWS)
    def _(i):
        forward_row(i, index, far, q, s.kv, s)

    for kind, owner in ((0, me.xm), (1, me.xp), (4, me.xm_z), (5, me.xp_z), (6, me.xo_z)):

        @pl.loop(0, OG_PARTS)
        def _(k):
            og_come(kind, owner, k)

        project_grad(owner, False, weight, s)

    @pl.loop(0, ROWS)
    def _(i):
        s.g[i, :, :2 * HD] = s.slots[i].astype(jnp.bfloat16)
        s.g[i, :, 2 * HD:] = s.slots[ROWS + i].astype(jnp.bfloat16)

    @pl.loop(0, OG_PARTS)
    def _(k):
        for kind, owner, to in og_kinds:
            og_gone(kind, owner, k)

    @pl.loop(0, KV_PARTS)
    def _(k):
        for kind, owner, to in kv_kinds:
            kv_gone(kind, owner, k)

    lo_kinds = [
        (0, me.xo_z, me.zp), (1, me.xp_z, me.xp), (2, me.xm_z, me.xm),
        (3, me.xp, me.xp), (4, me.xm, me.xm), (5, me.xo, me.xo), (6, me.zp, me.zp),
    ]

    def lo_piece(owner, k):
        return s.og.at[owner, pl.ds(k * OG_ROWS, OG_ROWS)]

    def lo_slot(kind, k):
        return s.lo.at[kind, pl.ds(k * OG_ROWS, OG_ROWS)]

    def lo_start(kind, k):
        _, owner, to = lo_kinds[kind]
        send(lo_piece(owner, k), lo_slot(kind, k), s.lo_send.at[kind, k], s.lo_recv.at[kind, k], me.on_head(to))

    def lo_come(kind, k):
        arrived(lo_slot(kind, k), s.lo_recv.at[kind, k], me.on_head(me.zp))
        return lo_slot(kind, k)[...].astype(jnp.float32)

    def share(owner, k):
        cols = pl.ds(pl.multiple_of(owner * NG * HD, NG * HD), NG * HD)
        rows = s.att[pl.ds(k * OG_ROWS, OG_ROWS)].reshape(OG_ROWS * BLK, NG * HD)
        out = dot(rows, weight[:, cols], 1, 0).astype(jnp.bfloat16)
        s.og[owner, pl.ds(k * OG_ROWS, OG_ROWS)] = out.reshape(OG_ROWS, BLK, NG * HD)

    @pl.loop(0, OG_PARTS)
    def _(k):
        for kind in range(5):
            share(lo_kinds[kind][1], k)
            lo_start(kind, k)
        share(me.xo, k)
        share(me.zp, k)
        share(me.h, k)

    def lo_pass(k):
        at = pl.ds(k * OG_ROWS, OG_ROWS)
        s.og[me.xo, at] = (s.og[me.xo, at].astype(jnp.float32) + lo_come(0, k)).astype(jnp.bfloat16)
        lo_start(5, k)
        total = s.og[me.zp, at].astype(jnp.float32) + lo_come(1, k) + lo_come(2, k)
        s.og[me.zp, at] = total.astype(jnp.bfloat16)
        lo_start(6, k)

    def lo_final(k):
        at = pl.ds(k * OG_ROWS, OG_ROWS)
        total = s.og[me.h, at].astype(jnp.float32)
        for kind in (3, 4, 5, 6):
            total = total + lo_come(kind, k)
        layer_out[at] = total.astype(jnp.bfloat16)

    def kv_first(i):
        @pl.loop(0, n_ctx // 2)
        def _(j):
            u = i * n_ctx + 2 * j + 1 - me.core
            s.s1[i, j] = collect(i, u, where, s).astype(jnp.bfloat16)

        send(s.s1.at[i], s.r1.at[i], s.send1.at[i], s.recv1.at[i], me.on_ctx(me.sib))

    def kv_second(i):
        arrived(s.r1.at[i], s.recv1.at[i], me.on_ctx(me.sib))

        @pl.loop(0, n_ctx // 2)
        def _(j):
            u = i * n_ctx + 2 * j + me.core
            s.s2[i, j] = (collect(i, u, where, s) + s.r1[i, j].astype(jnp.float32)).astype(jnp.bfloat16)

        for kind, to in enumerate((me.yp, me.ym, me.yo)):
            src = s.s2.at[i, pl.ds(2 * me.ys[kind], 2)]
            send(src, s.r2.at[i, kind], s.send2.at[i, kind], s.recv2.at[i, kind], me.on_ctx(to))

    def kv_sum(i, zh):
        total = s.s2[i, 2 * me.y + zh].astype(jnp.float32)
        for kind in range(3):
            total = total + s.r2[i, kind, zh].astype(jnp.float32)
        return total

    def kv_third(i):
        for kind in range(3):
            arrived(s.r2.at[i, kind], s.recv2.at[i, kind], me.on_ctx(me.sib))
        s.s3[i] = kv_sum(i, 1 - me.zh).astype(jnp.bfloat16)
        send(s.s3.at[i], s.r3.at[i], s.send3.at[i], s.recv3.at[i], me.on_ctx(me.zhp))

    def kv_final(i):
        arrived(s.r3.at[i], s.recv3.at[i], me.on_ctx(me.sib))
        total = kv_sum(i, me.zh) + s.r3[i].astype(jnp.float32)
        dk[i] = (total[:, :HD] * SCALE).astype(jnp.bfloat16)
        dv[i] = total[:, HD:].astype(jnp.bfloat16)

    @pl.loop(0, ROWS + 3)
    def _(n):
        i = ROWS - 1 - n

        @pl.when(n < ROWS)
        def _():
            backward_row(i, index, s.g, s.kv, s)
            kv_first(i)

        @pl.when((n >= 1) & (n <= ROWS))
        def _():
            kv_second(i + 1)

        @pl.when((n >= 2) & (n <= ROWS + 1))
        def _():
            kv_third(i + 2)

        @pl.when(n >= 3)
        def _():
            kv_final(i + 3)

        @pl.when((n >= 1) & (n <= OG_PARTS))
        def _():
            lo_pass(n - 1)

        @pl.when((n >= ROWS + 3 - OG_PARTS))
        def _():
            lo_final(n - (ROWS + 3 - OG_PARTS))

    @pl.loop(0, OG_PARTS)
    def _(k):
        for kind, owner, to in lo_kinds:
            sent(lo_piece(owner, k), s.lo_send.at[kind, k], me.on_head(to))

    @pl.loop(0, ROWS)
    def _(i):
        sent(s.s1.at[i], s.send1.at[i], me.on_ctx(me.sib))
        for kind in range(3):
            sent(s.s2.at[i, pl.ds(0, 2)], s.send2.at[i, kind], me.on_ctx(me.sib))
        sent(s.s3.at[i], s.send3.at[i], me.on_ctx(me.zhp))


def layer(index, far, where, q, key, value, out_grad, weight, n_head, n_ctx):
    smem = pl.BlockSpec(memory_space=pltpu.SMEM)
    vmem = pl.BlockSpec(memory_space=pltpu.VMEM)
    wide, narrow = (ROWS, BLK, NG * HD), (ROWS, BLK, HD)
    low = jnp.bfloat16
    sem = pltpu.SemaphoreType.DMA
    return pl.pallas_call(
        functools.partial(layer_kernel, n_ctx),
        out_shape=[jax.ShapeDtypeStruct(shape, low) for shape in (wide, wide, narrow, narrow)],
        in_specs=[smem] * 3 + [vmem] * 5,
        out_specs=[vmem] * 4,
        scratch_shapes=[
            pltpu.VMEM((ROWS, QN, HD), low),
            pltpu.VMEM((NCH, CK, 2 * HD), low),
            pltpu.VMEM((NCH, CK, QN), jnp.float32),
            pltpu.VMEM((CHUNKS, CK, QN), low),
            pltpu.VMEM((ROWS, HD, QN), low),
            pltpu.VMEM((ROWS, 8, QN), jnp.float32),
            pltpu.VMEM((HD, QN), low),
            pltpu.VMEM((QN, HD), low),
            pltpu.VMEM((NOSLOT + 1, BLK, 2 * HD), jnp.float32),
            pltpu.VMEM(wide, low),
            pltpu.VMEM(wide, low),
            pltpu.VMEM((n_ctx * ROWS, BLK, 2 * HD), low),
            pltpu.VMEM((n_head,) + wide, low),
            pltpu.VMEM((7,) + wide, low),
            pltpu.VMEM((ROWS, n_ctx // 2, BLK, 2 * HD), low),
            pltpu.VMEM((ROWS, n_ctx // 2, BLK, 2 * HD), low),
            pltpu.VMEM((ROWS, n_ctx // 2, BLK, 2 * HD), low),
            pltpu.VMEM((ROWS, 3, 2, BLK, 2 * HD), low),
            pltpu.VMEM((ROWS, BLK, 2 * HD), low),
            pltpu.VMEM((ROWS, BLK, 2 * HD), low),
            sem((7, OG_PARTS)), sem((7, OG_PARTS)),
            sem((15, KV_PARTS)), sem((15, KV_PARTS)),
            sem((7, OG_PARTS)), sem((7, OG_PARTS)),
            sem((ROWS,)), sem((ROWS,)),
            sem((ROWS, 3)), sem((ROWS, 3)),
            sem((ROWS,)), sem((ROWS,)),
        ],
        compiler_params=pltpu.CompilerParams(
            vmem_limit_bytes=63 << 20, collective_id=0, has_side_effects=True
        ),
        name="layer",
    )(index, far, where, q, key, value, out_grad, weight)


def on_device(query, key, value, out_grad, weight, vertical, slash):
    n_head, n_ctx = lax.axis_size("head"), lax.axis_size("ctx")
    index, far, where = lists(vertical[0, :, 0], slash[0, :, 0], lax.axis_index("ctx"), n_ctx)
    outs = layer(
        index, far, where, query[:, 0], key[:, 0], value[:, 0], out_grad[:, 0], weight, n_head, n_ctx
    )
    return tuple(x[:, None] for x in outs)


def solution(mesh):
    spread = P(None, "ctx", None, "head")
    listed = P("head", None, "ctx", None)
    return jax.shard_map(
        on_device,
        mesh=mesh,
        in_specs=(spread, spread, spread, spread, P("head", None), listed, listed),
        out_specs=(spread,) * 4,
        check_vma=False,
    )
```

```python
import functools
import math

import jax
import jax.numpy as jnp
from jax import lax
from jax.experimental import pallas as pl
from jax.experimental.pallas import tpu as pltpu
from jax.sharding import PartitionSpec as P

HD = 128
NG = 4
BLK = 64
ROWS = 8
NE = 40
EPC = 8
CK = EPC * BLK
NCH = NE // EPC
QN = NG * BLK
CHUNKS = 36
NOSLOT = CHUNKS * EPC
SCALE = 1.0 / math.sqrt(HD)
LOG2E = 1.4426950408889634
FAR = -1e30


def chunk_base(i):
    return jnp.where(i == 0, 0, jnp.where(i == 1, 2, 5 * i - 4))


def lists(vertical, slash, me, n_ctx):
    rows = jnp.arange(ROWS, dtype=jnp.int32)
    bid = rows * n_ctx + me
    raw = jnp.concatenate([bid[:, None] - slash, vertical], axis=1)
    kept = (raw >= 0) & (raw <= bid[:, None])
    order = jnp.arange(NE, dtype=jnp.int32)
    place = jnp.sum((kept[:, None, :] & (order[None, None, :] < order[None, :, None])).astype(jnp.int32), axis=2)
    place = jnp.where(kept, place, NE)
    here = place[:, None, :] == order[None, :, None]
    moved = raw % n_ctx * ROWS + raw // n_ctx
    index = jnp.sum(jnp.where(here, moved[:, None, :], 0), axis=2)
    far = jnp.where(jnp.any(here, axis=2), 0.0, FAR).astype(jnp.float32)
    slot = chunk_base(rows)[:, None] * EPC + place
    block = jnp.arange(ROWS * n_ctx, dtype=jnp.int32)
    hit = (raw[:, None, :] == block[None, :, None]) & kept[:, None, :]
    where = NOSLOT + jnp.sum(jnp.where(hit, slot[:, None, :] - NOSLOT, 0), axis=2)
    return index, far, where


def dot(a, b, ca, cb):
    return lax.dot_general(a, b, (((ca,), (cb,)), ((), ())), preferred_element_type=jnp.float32)


def heads_down(x):
    return jnp.concatenate([x[:, h * HD:(h + 1) * HD] for h in range(NG)], axis=0)


def heads_across(x):
    return jnp.concatenate([x[h * BLK:(h + 1) * BLK] for h in range(NG)], axis=1)


def forward_row(i, count, index, far, q, s):
    qs = heads_down(q[i])
    s.qs[i] = qs
    base = chunk_base(i)
    key_pos = lax.broadcasted_iota(jnp.int32, (BLK, QN), 0)
    query_pos = lax.broadcasted_iota(jnp.int32, (BLK, QN), 1) % BLK
    top = jnp.full((8, QN), FAR, jnp.float32)
    for ch in range(count):
        for e in range(EPC):
            s.kvrow[ch, e * BLK:(e + 1) * BLK, :] = s.table[index[i, ch * EPC + e]]
        sc = dot(s.kvrow[ch, :, :HD], qs, 1, 1)
        for e in range(EPC):
            part = sc[e * BLK:(e + 1) * BLK]
            if ch == 0 and e == 0:
                part = jnp.where(key_pos <= query_pos, part, FAR)
            s.sc[ch, e * BLK:(e + 1) * BLK, :] = part
            part = jnp.max(part.reshape(BLK // 8, 8, QN), axis=0)
            top = jnp.maximum(top, part + far[i, ch * EPC + e])
    top = jnp.max(top, axis=0, keepdims=True) * (SCALE * LOG2E)

    total = jnp.zeros((8, QN), jnp.float32)
    acc = jnp.zeros((HD, QN), jnp.float32)
    for ch in range(count):
        for e in range(EPC):
            shift = top - far[i, ch * EPC + e]
            p = jnp.exp2(s.sc[ch, e * BLK:(e + 1) * BLK, :] * (SCALE * LOG2E) - shift)
            total = total + jnp.sum(p.reshape(BLK // 8, 8, QN), axis=0)
            s.p[base + ch, e * BLK:(e + 1) * BLK, :] = p.astype(jnp.bfloat16)
        acc = acc + dot(s.kvrow[ch, :, HD:], s.p[base + ch], 0, 0)
    inv = 1.0 / jnp.sum(total, axis=0, keepdims=True)
    out = (acc * inv).astype(jnp.bfloat16)
    s.ot[i] = out
    s.inv[i] = jnp.broadcast_to(inv, (8, QN))
    s.att[i] = heads_across(out.astype(jnp.float32).T.astype(jnp.bfloat16))


def backward_row(i, count, index, s):
    base = chunk_base(i)
    gt = heads_down(s.g[i].astype(jnp.float32)).T
    gt = (gt * s.inv[i][0:1]).astype(jnp.bfloat16)
    g32 = gt.astype(jnp.float32)
    delta = jnp.sum(g32 * s.ot[i].astype(jnp.float32), axis=0, keepdims=True)
    gs = g32.T.astype(jnp.bfloat16)
    qs = s.qs[i]
    acc = jnp.zeros((HD, QN), jnp.float32)
    for ch in range(count):
        for e in range(EPC):
            s.kvrow[ch, e * BLK:(e + 1) * BLK, :] = s.table[index[i, ch * EPC + e]]
        dp = dot(s.kvrow[ch, :, HD:], gt, 1, 0)
        p = s.p[base + ch]
        ds = (p.astype(jnp.float32) * (dp - delta)).astype(jnp.bfloat16)
        at = pl.ds((base + ch) * EPC, EPC)
        s.slots[at, :, :HD] = dot(ds, qs, 1, 0).astype(jnp.bfloat16).reshape(EPC, BLK, HD)
        s.slots[at, :, HD:] = dot(p, gs, 1, 0).astype(jnp.bfloat16).reshape(EPC, BLK, HD)
        acc = acc + dot(s.kvrow[ch, :, :HD], ds, 0, 0)
    s.dq[i] = heads_across((acc * SCALE).T).astype(jnp.bfloat16)


def collect(i, u, where, s):
    def more(r, acc):
        return acc + s.slots[where[r, u]].astype(jnp.float32)

    return lax.fori_loop(i, ROWS, more, jnp.zeros((BLK, 2 * HD), jnp.float32))


class Scratch:
    pass


MESH = pl.DeviceIdType.MESH
OG_PARTS = 4
OG_ROWS = ROWS // OG_PARTS
HELD = 4
KV_PARTS = 4
KV_ROWS = ROWS // KV_PARTS


def send(src, dst, send_sem, recv_sem, device):
    pltpu.make_async_remote_copy(
        src_ref=src, dst_ref=dst, send_sem=send_sem, recv_sem=recv_sem, device_id=device, device_id_type=MESH
    ).start()


def sent(src, sem, device):
    pltpu.make_async_remote_copy(
        src_ref=src, dst_ref=src, send_sem=sem, recv_sem=sem, device_id=device, device_id_type=MESH
    ).wait_send()


def arrived(dst, sem, device):
    pltpu.make_async_remote_copy(
        src_ref=dst, dst_ref=dst, send_sem=sem, recv_sem=sem, device_id=device, device_id_type=MESH
    ).wait_recv()


class Place:
    def __init__(self):
        h, c = lax.axis_index("head"), lax.axis_index("ctx")
        self.h, self.c = h, c
        x, zl = h // 2, h % 2
        y, zh, core = c // 4, c // 2 % 2, c % 2
        self.y, self.zh, self.core = y, zh, core
        self.xp, self.xm, self.xo = [(x + k) % 4 * 2 + zl for k in (1, 3, 2)]
        self.zp = x * 2 + 1 - zl
        flip = 1 - 2 * zl
        self.xp_z, self.xm_z, self.xo_z = self.xp + flip, self.xm + flip, self.xo + flip
        self.ys = [(y + k) % 4 for k in (1, 3, 2)]
        self.yp, self.ym, self.yo = [v * 4 + zh * 2 + core for v in self.ys]
        turn = 2 * (1 - 2 * zh)
        self.zhp = c + turn
        self.yp_z, self.ym_z, self.yo_z = self.yp + turn, self.ym + turn, self.yo + turn
        self.other = 1 - 2 * core
        self.sib = c + self.other

    def on_head(self, index):
        return (index, self.c)

    def on_ctx(self, index):
        return (self.h, index)


def gather_out_grad(me, s):
    def piece(owner, k):
        return s.og.at[owner, pl.ds(k * OG_ROWS, OG_ROWS)]

    def go(kind, owner, to, k):
        ref = piece(owner, k)
        send(ref, ref, s.og_send.at[kind, k], s.og_recv.at[kind, k], me.on_head(to))

    def come(kind, owner, k):
        arrived(piece(owner, k), s.og_recv.at[kind, k], me.on_head(me.zp))

    def gone(kind, owner, k):
        sent(piece(owner, k), s.og_send.at[kind, k], me.on_head(me.zp))

    return go, come, gone


def gather_kv(me, s):
    def piece(owner, k):
        return s.kv.at[pl.ds(owner * ROWS + k * KV_ROWS, KV_ROWS)]

    def go(kind, owner, to, k):
        ref = piece(owner, k)
        send(ref, ref, s.kv_send.at[kind, k], s.kv_recv.at[kind, k], me.on_ctx(to))

    def come(kind, owner, k):
        arrived(piece(owner, k), s.kv_recv.at[kind, k], me.on_ctx(me.sib))

    def gone(kind, owner, k):
        sent(piece(owner, k), s.kv_send.at[kind, k], me.on_ctx(me.sib))

    return go, come, gone


def layer_kernel(n_ctx, index, far, where, q, key, value, out_grad, weight, layer_out, dq, dk, dv, *refs):
    s = Scratch()
    (
        s.qs, s.kvrow, s.sc, s.p, s.ot, s.inv, s.slots, s.att, s.g, s.weight, s.kv, s.table, s.og,
        s.ls, s.lo, s.s1, s.r1, s.s2, s.r2, s.s3, s.r3, w_sem,
        s.og_send, s.og_recv, s.kv_send, s.kv_recv, s.lo_send, s.lo_recv,
        s.send1, s.recv1, s.send2, s.recv2, s.send3, s.recv3, s.send4, s.recv4,
    ) = refs
    s.dq = dq
    me = Place()
    w_copy = pltpu.make_async_copy(weight, s.weight, w_sem)
    w_copy.start()
    mine = pl.multiple_of(me.c * ROWS, ROWS)
    s.kv[pl.ds(mine, ROWS), :, :HD] = key[...]
    s.kv[pl.ds(mine, ROWS), :, HD:] = value[...]
    s.og[me.h] = out_grad[...]

    barrier = pltpu.get_barrier_semaphore()
    partners = [me.on_head(d) for d in (me.xp, me.xm, me.xo, me.zp)]
    partners += [me.on_ctx(d) for d in (me.zhp, me.yp, me.ym, me.yo, me.sib)]
    for device in partners:
        pl.semaphore_signal(barrier, inc=1, device_id=device, device_id_type=MESH)
    pl.semaphore_wait(barrier, len(partners))

    og_go, og_come, og_gone = gather_out_grad(me, s)
    kv_go, kv_come, kv_gone = gather_kv(me, s)
    kv_kinds = [
        (0, me.c, me.yp), (1, me.c, me.ym), (2, me.c, me.yo), (3, me.c, me.zhp),
        (4, me.zhp, me.yp), (5, me.zhp, me.ym), (6, me.yo, me.zhp),
        (7, me.c, me.sib), (8, me.zhp, me.sib), (9, me.ym, me.sib), (10, me.yp, me.sib), (11, me.yo, me.sib),
        (12, me.ym_z, me.sib), (13, me.yp_z, me.sib), (14, me.yo_z, me.sib),
    ]
    og_kinds = {
        0: (0, me.h, me.xp), 1: (1, me.h, me.xm), 3: (3, me.h, me.zp),
        4: (4, me.zp, me.xp), 5: (5, me.zp, me.xm), 6: (6, me.xo, me.zp),
    }

    def kv_start(kinds, k):
        for kind in kinds:
            kv_go(*kv_kinds[kind], k)

    def og_start(kinds, k):
        for kind in kinds:
            og_go(*og_kinds[kind], k)

    def og_across(k):
        og_come(0, me.xm, k)
        og_come(1, me.xp, k)
        og_go(2, me.xm if k % 2 == 0 else me.xp, me.xp if k % 2 == 0 else me.xm, k)

    def og_near(k):
        og_come(3, me.zp, k)
        og_start((4, 5), k)

    def og_far(k):
        og_come(2, me.xo, k)
        og_start((6,), k)

    def kv_pass(k):
        kv_come(3, me.zhp, k)
        kv_start((4, 5, 8), k)

    def kv_near(k):
        for kind, owner in ((0, me.ym), (1, me.yp), (2, me.yo)):
            kv_come(kind, owner, k)
        kv_start((6, 9, 10, 11), k)

    def kv_far(k):
        for kind, owner in ((4, me.ym_z), (5, me.yp_z), (6, me.yo_z)):
            kv_come(kind, owner, k)
        kv_start((12, 13, 14), k)

    def kv_ready(k):
        owners = (me.c, me.zhp, me.ym, me.yp, me.yo, me.ym_z, me.yp_z, me.yo_z)
        for kind, owner in enumerate(owners, 7):
            kv_come(kind, owner + me.other, k)

        @pl.loop(0, n_ctx)
        def _(c):
            at = pl.ds(c * ROWS + k * KV_ROWS, KV_ROWS)
            s.table[at] = s.kv[at]

    for k in range(KV_PARTS):
        kv_start((3,), k)
    for k in range(KV_PARTS):
        kv_start((0, 1, 2, 7), k)
        og_start((0, 1), OG_PARTS - 1 - k)
    og_start((3,), 3)
    og_start((3,), 2)
    s.slots[NOSLOT] = jnp.zeros((BLK, 2 * HD), jnp.bfloat16)
    kv_pass(0)
    og_across(3)
    kv_near(0)
    kv_pass(1)
    og_across(2)
    kv_near(1)
    og_start((3,), 1)
    kv_pass(2)
    kv_pass(3)
    og_across(1)
    kv_near(2)
    og_start((3,), 0)
    og_near(3)
    og_across(0)
    kv_near(3)
    kv_far(0)
    og_near(2)
    kv_ready(0)
    w_copy.wait()

    lo_kinds = [
        (0, me.xo_z, me.zp), (1, me.xp_z, me.xp), (2, me.xm_z, me.xm),
        (3, me.xp, me.xp), (4, me.xm, me.xm), (5, me.xo, None), (6, me.zp, me.zp),
    ]

    def lo_piece(owner, k):
        return s.ls.at[owner, pl.ds(k * OG_ROWS, OG_ROWS)]

    def lo_slot(kind, k):
        return s.lo.at[kind, pl.ds(k * OG_ROWS, OG_ROWS)]

    def lo_start(kind, k):
        _, owner, to = lo_kinds[kind]
        if to is None:
            to = jnp.where(k % 2 == 0, me.xm, me.xp)
        send(lo_piece(owner, k), lo_slot(kind, k), s.lo_send.at[kind, k], s.lo_recv.at[kind, k], me.on_head(to))

    def lo_come(kind, k):
        arrived(lo_slot(kind, k), s.lo_recv.at[kind, k], me.on_head(me.zp))
        return lo_slot(kind, k)[...].astype(jnp.float32)

    def lo_add(owner, k, kinds):
        at = pl.ds(k * OG_ROWS, OG_ROWS)
        total = s.ls[owner, at].astype(jnp.float32)
        for kind in kinds:
            total = total + lo_come(kind, k)
        return total.astype(jnp.bfloat16)

    def share(owner, k):
        cols = pl.ds(pl.multiple_of(owner * NG * HD, NG * HD), NG * HD)
        rows = s.att[pl.ds(k * OG_ROWS, OG_ROWS)].reshape(OG_ROWS * BLK, NG * HD)
        out = dot(rows, s.weight[:, cols], 1, 0).astype(jnp.bfloat16)
        s.ls[owner, pl.ds(k * OG_ROWS, OG_ROWS)] = out.reshape(OG_ROWS, BLK, NG * HD)

    def shares(k):
        for kind in range(5):
            share(lo_kinds[kind][1], k)
            if kind < 3:
                lo_start(kind, k)
        even = k % 2 == 0

        @pl.when(even)
        def _():
            lo_start(3, k)

        @pl.when(jnp.logical_not(even))
        def _():
            lo_start(4, k)

        share(me.xo, k)
        share(me.zp, k)
        share(me.h, k)

    def lo_pass(k):
        at = pl.ds(k * OG_ROWS, OG_ROWS)
        s.ls[me.xo, at] = lo_add(me.xo, k, (0,))
        lo_start(5, k)
        s.ls[me.zp, at] = lo_add(me.zp, k, (1, 2))
        lo_start(6, k)

    def lo_last(k):
        at = pl.ds(k * OG_ROWS, OG_ROWS)
        even = k % 2 == 0
        owner = jnp.where(even, me.xm, me.xp)
        s.ls[owner, at] = lo_add(owner, k, (5,))

        @pl.when(even)
        def _():
            lo_start(4, k)

        @pl.when(jnp.logical_not(even))
        def _():
            lo_start(3, k)

    def lo_final(k):
        layer_out[pl.ds(k * OG_ROWS, OG_ROWS)] = lo_add(me.h, k, (3, 4, 6))

    forward_row(0, 2, index, far, q, s)
    kv_far(1)
    og_near(1)
    og_far(3)
    forward_row(1, 4, index, far, q, s)
    shares(0)

    @pl.loop(1, KV_PARTS)
    def _(k):
        kv_ready(k)

        @pl.loop(0, 2)
        def _(half):
            @pl.when((half == 1) & (k < KV_PARTS - 1))
            def _():
                kv_far(k + 1)

            @pl.when((half == 1) & (k == 1))
            def _():
                og_near(0)

            @pl.when(half == 1)
            def _():
                og_far(KV_PARTS - 1 - k)

            forward_row(2 * k + half, NCH, index, far, q, s)

        shares(k)

    def og_ready(k):
        for kind, owner in ((4, me.xm_z), (5, me.xp_z), (6, me.xo_z)):
            og_come(kind, owner, k)

    def project_grad(k):
        at = pl.ds(k * OG_ROWS, OG_ROWS)
        total = None
        for owner in range(s.og.shape[0]):
            cols = slice(owner * NG * HD, (owner + 1) * NG * HD)
            part = dot(s.og[owner, at].reshape(OG_ROWS * BLK, NG * HD), s.weight[:, cols], 1, 1)
            total = part if total is None else total + part
        s.g[at] = total.astype(jnp.bfloat16).reshape(OG_ROWS, BLK, NG * HD)

    def kv_first(i):
        at = i % HELD

        @pl.when(i < ROWS - HELD)
        def _():
            sent(s.s1.at[at], s.send1.at[i + HELD], me.on_ctx(me.sib))

        @pl.loop(0, n_ctx // 2)
        def _(j):
            u = i * n_ctx + 2 * j + 1 - me.core
            s.s1[at, j] = collect(i, u, where, s).astype(jnp.bfloat16)

        send(s.s1.at[at], s.r1.at[i], s.send1.at[i], s.recv1.at[i], me.on_ctx(me.sib))

        @pl.loop(0, n_ctx // 2)
        def _(j):
            u = i * n_ctx + 2 * j + me.core
            s.s2[i, j] = collect(i, u, where, s).astype(jnp.bfloat16)

    def kv_second(i):
        arrived(s.r1.at[i], s.recv1.at[i], me.on_ctx(me.sib))
        s.s2[i] = (s.s2[i].astype(jnp.float32) + s.r1[i].astype(jnp.float32)).astype(jnp.bfloat16)
        for kind, to in enumerate((me.yp, me.ym)):
            src = s.s2.at[i, pl.ds(2 * me.ys[kind], 2)]
            send(src, s.r2.at[i, kind], s.send2.at[i, kind], s.recv2.at[i, kind], me.on_ctx(to))
        send(far_share(i, 1 - me.zh), s.r2.at[i, 2, 0], s.send4.at[i], s.recv4.at[i], me.on_ctx(me.zhp))

    def far_share(i, zh):
        return s.s2.at[i, 2 * me.ys[2] + zh]

    def kv_far_sum(i):
        arrived(s.r2.at[i, 2, 0], s.recv4.at[i], me.on_ctx(me.zhp))
        ref = far_share(i, me.zh)
        ref[...] = (ref[...].astype(jnp.float32) + s.r2[i, 2, 0].astype(jnp.float32)).astype(jnp.bfloat16)
        send(ref, s.r2.at[i, 2, 1], s.send2.at[i, 2], s.recv2.at[i, 2], me.on_ctx(me.yo))

    def kv_sum(i, zh):
        total = s.s2[i, 2 * me.y + zh].astype(jnp.float32)
        for kind in range(2):
            total = total + s.r2[i, kind, zh].astype(jnp.float32)
        return total

    def kv_third(i):
        kv_far_sum(i)
        for kind in range(2):
            arrived(s.r2.at[i, kind], s.recv2.at[i, kind], me.on_ctx(me.sib))
        s.s3[i] = kv_sum(i, 1 - me.zh).astype(jnp.bfloat16)
        send(s.s3.at[i], s.r3.at[i], s.send3.at[i], s.recv3.at[i], me.on_ctx(me.zhp))

    def kv_final(i):
        arrived(s.r3.at[i], s.recv3.at[i], me.on_ctx(me.sib))
        arrived(s.r2.at[i, 2, 1], s.recv2.at[i, 2], me.on_ctx(me.sib))
        total = kv_sum(i, me.zh) + s.r3[i].astype(jnp.float32) + s.r2[i, 2, 1].astype(jnp.float32)
        dk[i] = (total[:, :HD] * SCALE).astype(jnp.bfloat16)
        dv[i] = total[:, HD:].astype(jnp.bfloat16)

    def step(n, count):
        i = ROWS - 1 - n
        backward_row(i, count, index, s)
        kv_first(i)

        @pl.when(n >= 1)
        def _():
            kv_second(i + 1)

        @pl.when(n >= 3)
        def _():
            kv_third(i + 3)

        @pl.when(n >= 5)
        def _():
            kv_final(i + 5)

    @pl.loop(0, ROWS - 2)
    def _(n):
        @pl.when(n % 2 == 0)
        def _():
            og_ready(OG_PARTS - 1 - n // 2)
            project_grad(OG_PARTS - 1 - n // 2)

        step(n, NCH)

        @pl.when(n < OG_PARTS)
        def _():
            lo_pass(n)

        @pl.when(n >= 2)
        def _():
            lo_last(n - 2)

    og_ready(0)
    project_grad(0)
    step(ROWS - 2, 4)
    step(ROWS - 1, 2)
    kv_second(0)
    kv_third(2)
    lo_final(0)
    lo_final(1)
    kv_third(1)
    kv_final(4)
    kv_final(3)
    lo_final(2)
    kv_third(0)
    kv_final(2)
    kv_final(1)
    lo_final(3)
    kv_final(0)

    @pl.loop(0, OG_PARTS)
    def _(k):
        for kind, owner, to in og_kinds.values():
            og_gone(kind, owner, k)
        og_gone(2, me.xm, k)
        for kind, owner, to in lo_kinds:
            sent(lo_piece(owner, k), s.lo_send.at[kind, k], me.on_head(me.zp))

    @pl.loop(0, KV_PARTS)
    def _(k):
        for kind, owner, to in kv_kinds:
            kv_gone(kind, owner, k)

    @pl.loop(0, ROWS)
    def _(i):
        for kind in range(2):
            sent(s.s2.at[i, pl.ds(0, 2)], s.send2.at[i, kind], me.on_ctx(me.sib))
        sent(s.s2.at[i, 0], s.send2.at[i, 2], me.on_ctx(me.sib))
        sent(s.s2.at[i, 0], s.send4.at[i], me.on_ctx(me.sib))
        sent(s.s3.at[i], s.send3.at[i], me.on_ctx(me.zhp))

    @pl.loop(0, HELD)
    def _(i):
        sent(s.s1.at[i], s.send1.at[i], me.on_ctx(me.sib))


def hand_over_kernel(*refs):
    count = len(refs) // 2
    for k in range(count):
        refs[count + k][...] = refs[k][...]


def hand_over(arrays):
    vmem = pl.BlockSpec(memory_space=pltpu.VMEM)
    return pl.pallas_call(
        hand_over_kernel,
        out_shape=[jax.ShapeDtypeStruct(x.shape, x.dtype) for x in arrays],
        in_specs=[vmem] * len(arrays),
        out_specs=[vmem] * len(arrays),
        name="hand_over",
    )(*arrays)


def layer(index, far, where, q, key, value, out_grad, weight, n_head, n_ctx):
    smem = pl.BlockSpec(memory_space=pltpu.SMEM)
    vmem = pl.BlockSpec(memory_space=pltpu.VMEM)
    wide, narrow = (ROWS, BLK, NG * HD), (ROWS, BLK, HD)
    low = jnp.bfloat16
    sem = pltpu.SemaphoreType.DMA
    return pl.pallas_call(
        functools.partial(layer_kernel, n_ctx),
        out_shape=[jax.ShapeDtypeStruct(shape, low) for shape in (wide, wide, narrow, narrow)],
        in_specs=[smem] * 3 + [vmem] * 4 + [pl.BlockSpec(memory_space=pl.ANY)],
        out_specs=[vmem] * 4,
        scratch_shapes=[
            pltpu.VMEM((ROWS, QN, HD), low),
            pltpu.VMEM((NCH, CK, 2 * HD), low),
            pltpu.VMEM((NCH, CK, QN), jnp.float32),
            pltpu.VMEM((CHUNKS, CK, QN), low),
            pltpu.VMEM((ROWS, HD, QN), low),
            pltpu.VMEM((ROWS, 8, QN), jnp.float32),
            pltpu.VMEM((NOSLOT + 1, BLK, 2 * HD), low),
            pltpu.VMEM(wide, low),
            pltpu.VMEM(wide, low),
            pltpu.VMEM(weight.shape, low),
            pltpu.VMEM((n_ctx * ROWS, BLK, 2 * HD), low),
            pltpu.VMEM((n_ctx * ROWS, BLK, 2 * HD), low),
            pltpu.VMEM((n_head,) + wide, low),
            pltpu.VMEM((n_head,) + wide, low),
            pltpu.VMEM((7,) + wide, low),
            pltpu.VMEM((HELD, n_ctx // 2, BLK, 2 * HD), low),
            pltpu.VMEM((ROWS, n_ctx // 2, BLK, 2 * HD), low),
            pltpu.VMEM((ROWS, n_ctx // 2, BLK, 2 * HD), low),
            pltpu.VMEM((ROWS, 3, 2, BLK, 2 * HD), low),
            pltpu.VMEM((ROWS, BLK, 2 * HD), low),
            pltpu.VMEM((ROWS, BLK, 2 * HD), low),
            sem,
            sem((7, OG_PARTS)), sem((7, OG_PARTS)),
            sem((15, KV_PARTS)), sem((15, KV_PARTS)),
            sem((7, OG_PARTS)), sem((7, OG_PARTS)),
            sem((ROWS,)), sem((ROWS,)),
            sem((ROWS, 3)), sem((ROWS, 3)),
            sem((ROWS,)), sem((ROWS,)),
            sem((ROWS,)), sem((ROWS,)),
        ],
        compiler_params=pltpu.CompilerParams(
            vmem_limit_bytes=63 << 20, collective_id=0, has_side_effects=True
        ),
        name="layer",
    )(index, far, where, q, key, value, out_grad, weight)


def on_device(query, key, value, out_grad, weight, vertical, slash):
    n_head, n_ctx = lax.axis_size("head"), lax.axis_size("ctx")
    index, far, where = lists(vertical[0, :, 0], slash[0, :, 0], lax.axis_index("ctx"), n_ctx)
    outs = layer(
        index, far, where, query[:, 0], key[:, 0], value[:, 0], out_grad[:, 0], weight, n_head, n_ctx
    )
    return tuple(x[:, None] for x in hand_over(outs))


def solution(mesh):
    spread = P(None, "ctx", None, "head")
    listed = P("head", None, "ctx", None)
    return jax.shard_map(
        on_device,
        mesh=mesh,
        in_specs=(spread, spread, spread, spread, P("head", None), listed, listed),
        out_specs=(spread,) * 4,
        check_vma=False,
    )
```

```python
import functools
import math

import jax
import jax.numpy as jnp
from jax import lax
from jax.experimental import pallas as pl
from jax.experimental.pallas import tpu as pltpu
from jax.sharding import PartitionSpec as P

HD = 128
NG = 4
BLK = 64
ROWS = 8
NE = 40
EPC = 8
CK = EPC * BLK
NCH = NE // EPC
QN = NG * BLK
CHUNKS = 36
NOSLOT = CHUNKS * EPC
SCALE = 1.0 / math.sqrt(HD)
LOG2E = 1.4426950408889634
FAR = -1e30


def chunk_base(i):
    return jnp.where(i == 0, 0, jnp.where(i == 1, 2, 5 * i - 4))


def lists(vertical, slash, me, n_ctx):
    rows = jnp.arange(ROWS, dtype=jnp.int32)
    bid = rows * n_ctx + me
    raw = jnp.concatenate([bid[:, None] - slash, vertical], axis=1)
    kept = (raw >= 0) & (raw <= bid[:, None])
    order = jnp.arange(NE, dtype=jnp.int32)
    place = jnp.sum((kept[:, None, :] & (order[None, None, :] < order[None, :, None])).astype(jnp.int32), axis=2)
    place = jnp.where(kept, place, NE)
    moved = raw % n_ctx * ROWS + raw // n_ctx
    slot = chunk_base(rows)[:, None] * EPC + place
    blocks = ROWS * n_ctx
    column = jnp.arange(NE + blocks + 1, dtype=jnp.int32)[None, :, None]
    by_place = place[:, None, :] == column
    by_block = kept[:, None, :] & (raw[:, None, :] == column - NE)
    last = column == NE + blocks
    picked = jnp.where(by_place & (column < NE), moved[:, None, :], 0)
    picked = jnp.where(by_block, slot[:, None, :] - NOSLOT, picked)
    picked = jnp.where(last, kept[:, None, :].astype(jnp.int32), picked)
    table = jnp.sum(picked, axis=2)
    block_column = (column[..., 0] >= NE) & (column[..., 0] < NE + blocks)
    return jnp.where(block_column, table + NOSLOT, table)


def dot(a, b, ca, cb):
    return lax.dot_general(a, b, (((ca,), (cb,)), ((), ())), preferred_element_type=jnp.float32)


def heads_down(x):
    return jnp.concatenate([x[:, h * HD:(h + 1) * HD] for h in range(NG)], axis=0)


def heads_across(x):
    return jnp.concatenate([x[h * BLK:(h + 1) * BLK] for h in range(NG)], axis=1)


def forward_row(i, count, index, q, s):
    qs = heads_down(q[i])
    s.qs[i] = qs
    base = chunk_base(i)
    key_pos = lax.broadcasted_iota(jnp.int32, (BLK, QN), 0)
    query_pos = lax.broadcasted_iota(jnp.int32, (BLK, QN), 1) % BLK
    top = jnp.full((8, QN), FAR, jnp.float32)
    entries = index[i, index.shape[1] - 1]

    def far(at):
        return jnp.where(at < entries, 0.0, FAR)

    for ch in range(count):
        for e in range(EPC):
            s.kvrow[ch, e * BLK:(e + 1) * BLK, :] = s.table[index[i, ch * EPC + e]]
        sc = dot(s.kvrow[ch, :, :HD], qs, 1, 1)
        for e in range(EPC):
            part = sc[e * BLK:(e + 1) * BLK]
            if ch == 0 and e == 0:
                part = jnp.where(key_pos <= query_pos, part, FAR)
            s.sc[ch, e * BLK:(e + 1) * BLK, :] = part
            part = jnp.max(part.reshape(BLK // 8, 8, QN), axis=0)
            top = jnp.maximum(top, part + far(ch * EPC + e))
    top = jnp.max(top, axis=0, keepdims=True) * (SCALE * LOG2E)

    total = jnp.zeros((8, QN), jnp.float32)
    acc = jnp.zeros((HD, QN), jnp.float32)
    for ch in range(count):
        for e in range(EPC):
            shift = top - far(ch * EPC + e)
            p = jnp.exp2(s.sc[ch, e * BLK:(e + 1) * BLK, :] * (SCALE * LOG2E) - shift)
            total = total + jnp.sum(p.reshape(BLK // 8, 8, QN), axis=0)
            s.p[base + ch, e * BLK:(e + 1) * BLK, :] = p.astype(jnp.bfloat16)
        acc = acc + dot(s.kvrow[ch, :, HD:], s.p[base + ch], 0, 0)
    inv = 1.0 / jnp.sum(total, axis=0, keepdims=True)
    out = (acc * inv).astype(jnp.bfloat16)
    s.ot[i] = out
    s.inv[i] = jnp.broadcast_to(inv, (8, QN))
    s.att[i] = heads_across(out.astype(jnp.float32).T.astype(jnp.bfloat16))


def backward_row(i, count, index, s):
    base = chunk_base(i)
    gt = heads_down(s.g[i].astype(jnp.float32)).T
    gt = (gt * s.inv[i][0:1]).astype(jnp.bfloat16)
    g32 = gt.astype(jnp.float32)
    delta = jnp.sum(g32 * s.ot[i].astype(jnp.float32), axis=0, keepdims=True)
    gs = g32.T.astype(jnp.bfloat16)
    qs = s.qs[i]
    for ch in range(count):
        for e in range(EPC):
            s.kvrow[ch, e * BLK:(e + 1) * BLK, HD:] = s.table[index[i, ch * EPC + e], :, HD:]
        dp = dot(s.kvrow[ch, :, HD:], gt, 1, 0)
        p = s.p[base + ch]
        ds = (p.astype(jnp.float32) * (dp - delta)).astype(jnp.bfloat16)
        at = pl.ds((base + ch) * EPC, EPC)
        s.slots[at, :, :HD] = dot(ds, qs, 1, 0).astype(jnp.bfloat16).reshape(EPC, BLK, HD)
        s.slots[at, :, HD:] = dot(p, gs, 1, 0).astype(jnp.bfloat16).reshape(EPC, BLK, HD)
        s.p[base + ch] = ds


def query_row(i, count, index, s):
    acc = jnp.zeros((HD, QN), jnp.float32)
    base = chunk_base(i)
    for ch in range(count):
        for e in range(EPC):
            s.kvrow[ch, e * BLK:(e + 1) * BLK, :HD] = s.table[index[i, ch * EPC + e], :, :HD]
        acc = acc + dot(s.kvrow[ch, :, :HD], s.p[base + ch], 0, 0)
    s.dq[i] = heads_across((acc * SCALE).T).astype(jnp.bfloat16)


def collect(first, u, index, s):
    total = s.slots[index[first, NE + u]].astype(jnp.float32)
    for r in range(first + 1, ROWS):
        total = total + s.slots[index[r, NE + u]].astype(jnp.float32)
    return total


def collect_row(i, core, n_ctx, index, s, out):
    for first in range(ROWS):

        @pl.when(i == first)
        def _():
            @pl.loop(0, n_ctx // 2)
            def _(j):
                out[j] = collect(first, first * n_ctx + 2 * j + core, index, s).astype(jnp.bfloat16)


class Scratch:
    pass


MESH = pl.DeviceIdType.MESH
OG_PARTS = 4
OG_ROWS = ROWS // OG_PARTS
HELD = 4
KV_PARTS = 4
OVER_Y = 2
KV_ROWS = ROWS // KV_PARTS


def send(src, dst, send_sem, recv_sem, device):
    pltpu.make_async_remote_copy(
        src_ref=src, dst_ref=dst, send_sem=send_sem, recv_sem=recv_sem, device_id=device, device_id_type=MESH
    ).start()


def sent(src, sem, device):
    pltpu.make_async_remote_copy(
        src_ref=src, dst_ref=src, send_sem=sem, recv_sem=sem, device_id=device, device_id_type=MESH
    ).wait_send()


def arrived(dst, sem, device):
    pltpu.make_async_remote_copy(
        src_ref=dst, dst_ref=dst, send_sem=sem, recv_sem=sem, device_id=device, device_id_type=MESH
    ).wait_recv()


class Place:
    def __init__(self):
        h, c = lax.axis_index("head"), lax.axis_index("ctx")
        self.h, self.c = h, c
        x, zl = h // 2, h % 2
        y, zh, core = c // 4, c // 2 % 2, c % 2
        self.y, self.zh, self.core = y, zh, core
        self.xp, self.xm, self.xo = [(x + k) % 4 * 2 + zl for k in (1, 3, 2)]
        self.zp = x * 2 + 1 - zl
        flip = 1 - 2 * zl
        self.xp_z, self.xm_z, self.xo_z = self.xp + flip, self.xm + flip, self.xo + flip
        self.ys = [(y + k) % 4 for k in (1, 3, 2)]
        self.yp, self.ym, self.yo = [v * 4 + zh * 2 + core for v in self.ys]
        turn = 2 * (1 - 2 * zh)
        self.zhp = c + turn
        self.yp_z, self.ym_z, self.yo_z = self.yp + turn, self.ym + turn, self.yo + turn
        self.other = 1 - 2 * core
        self.sib = c + self.other

    def on_head(self, index):
        return (index, self.c)

    def on_ctx(self, index):
        return (self.h, index)


def gather_out_grad(me, s):
    def piece(owner, k):
        return s.og.at[owner, pl.ds(k * OG_ROWS, OG_ROWS)]

    def go(kind, owner, to, k):
        ref = piece(owner, k)
        send(ref, ref, s.og_send.at[kind, k], s.og_recv.at[kind, k], me.on_head(to))

    def come(kind, owner, k):
        arrived(piece(owner, k), s.og_recv.at[kind, k], me.on_head(me.zp))

    def gone(kind, owner, k):
        sent(piece(owner, k), s.og_send.at[kind, k], me.on_head(me.zp))

    return go, come, gone


def gather_kv(me, s):
    def piece(owner, k):
        return s.kv.at[pl.ds(owner * ROWS + k * KV_ROWS, KV_ROWS)]

    def go(kind, owner, to, k):
        ref = piece(owner, k)
        send(ref, ref, s.kv_send.at[kind, k], s.kv_recv.at[kind, k], me.on_ctx(to))

    def come(kind, owner, k):
        arrived(piece(owner, k), s.kv_recv.at[kind, k], me.on_ctx(me.sib))

    def gone(kind, owner, k):
        sent(piece(owner, k), s.kv_send.at[kind, k], me.on_ctx(me.sib))

    return go, come, gone


def layer_kernel(n_ctx, index, q, key, value, out_grad, weight, layer_out, dq, dk, dv, *refs):
    s = Scratch()
    (
        s.qs, s.kvrow, s.sc, s.p, s.ot, s.inv, s.slots, s.att, s.g, s.acc, s.weight, s.kv, s.table, s.og,
        s.ls, s.lo, s.s1, s.r1, s.s2, s.r2, s.s3, s.r3, w_sem,
        s.og_send, s.og_recv, s.kv_send, s.kv_recv, s.lo_send, s.lo_recv,
        s.send1, s.recv1, s.send2, s.recv2, s.send3, s.recv3, s.send4, s.recv4, s.send5, s.recv5,
    ) = refs
    s.dq = dq
    me = Place()
    w_copy = pltpu.make_async_copy(weight, s.weight, w_sem)
    w_copy.start()
    mine = pl.multiple_of(me.c * ROWS, ROWS)
    s.kv[pl.ds(mine, ROWS), :, :HD] = key[...]
    s.kv[pl.ds(mine, ROWS), :, HD:] = value[...]
    s.og[me.h] = out_grad[...]

    barrier = pltpu.get_barrier_semaphore()
    partners = [me.on_head(d) for d in (me.xp, me.xm, me.xo, me.zp)]
    column = (me.yp, me.ym, me.yo, me.yp_z, me.ym_z, me.yo_z, me.zhp)
    partners += [me.on_ctx(d) for d in column + (me.sib,)]
    for device in partners:
        pl.semaphore_signal(barrier, inc=1, device_id=device, device_id_type=MESH)
    pl.semaphore_wait(barrier, len(partners))

    og_go, og_come, og_gone = gather_out_grad(me, s)
    kv_go, kv_come, kv_gone = gather_kv(me, s)
    kv_kinds = [
        (0, me.c, me.yp), (1, me.c, me.ym), (2, me.c, me.yo), (3, me.c, me.zhp),
        (4, me.zhp, me.yp), (5, me.zhp, me.ym), (6, me.zhp, me.yo),
        (7, me.c, me.sib), (8, me.zhp, me.sib), (9, me.ym, me.sib), (10, me.yp, me.sib), (11, me.yo, me.sib),
        (12, me.ym_z, me.sib), (13, me.yp_z, me.sib), (14, me.yo_z, me.sib),
    ]
    og_kinds = {
        0: (0, me.h, me.xp), 1: (1, me.h, me.xm), 3: (3, me.h, me.zp),
        4: (4, me.zp, me.xp), 5: (5, me.zp, me.xm), 6: (6, me.xo, me.zp),
    }

    def kv_start(kinds, k):
        for kind in kinds:
            kv_go(*kv_kinds[kind], k)

    def og_start(kinds, k):
        for kind in kinds:
            og_go(*og_kinds[kind], k)

    def og_across(k):
        og_come(0, me.xm, k)
        og_come(1, me.xp, k)
        og_go(2, me.xm if k % 2 == 0 else me.xp, me.xp if k % 2 == 0 else me.xm, k)

    def og_near(k):
        og_come(3, me.zp, k)
        og_start((4, 5), k)

    def og_far(k):
        og_come(2, me.xo, k)
        og_start((6,), k)

    def project_early(owner, first):
        cols = pl.ds(pl.multiple_of(owner * NG * HD, NG * HD), NG * HD)
        part = dot(s.og[owner].reshape(ROWS * BLK, NG * HD), s.weight[:, cols], 1, 1)
        part = part.reshape(ROWS, BLK, NG * HD)
        s.acc[...] = part if first else s.acc[...] + part

    def kv_pass(k):
        kv_come(3, me.zhp, k)
        if k < OVER_Y:
            kv_start((6,), k)
        kv_start((4, 5, 8), k)

    def kv_near(k):
        for kind, owner in ((0, me.ym), (1, me.yp), (2, me.yo)):
            kv_come(kind, owner, k)
        if k >= OVER_Y:
            kv_go(6, me.yo, me.zhp, k)
        kv_start((9, 10, 11), k)

    def kv_far(k):
        for kind, owner in ((4, me.ym_z), (5, me.yp_z), (6, me.yo_z)):
            kv_come(kind, owner, k)
        kv_start((12, 13, 14), k)

    def kv_ready(k):
        owners = (me.c, me.zhp, me.ym, me.yp, me.yo, me.ym_z, me.yp_z, me.yo_z)
        for kind, owner in enumerate(owners, 7):
            kv_come(kind, owner + me.other, k)

        @pl.loop(0, n_ctx)
        def _(c):
            at = pl.ds(c * ROWS + k * KV_ROWS, KV_ROWS)
            s.table[at] = s.kv[at]

    for k in range(KV_PARTS):
        kv_start((3,), k)
    for k in range(2):
        kv_start((2, 0, 1, 7), k)
        og_start((0, 1), OG_PARTS - 1 - k)
    og_start((3,), 3)
    og_start((3,), 2)
    og_start((0, 1), 1)
    og_start((0, 1), 0)
    s.slots[NOSLOT] = jnp.zeros((BLK, 2 * HD), jnp.bfloat16)
    kv_pass(0)
    kv_start((2, 0, 1, 7), 2)
    og_across(3)
    kv_pass(1)
    kv_start((2, 0, 1, 7), 3)
    kv_near(0)
    kv_pass(2)
    og_across(2)
    kv_pass(3)
    og_start((3,), 1)
    og_start((3,), 0)
    kv_near(1)
    og_across(1)
    og_near(3)
    kv_far(0)
    og_across(0)
    og_near(2)
    w_copy.wait()
    for owner in (me.h, me.xm, me.xp):
        project_early(owner, owner is me.h)
    kv_ready(0)

    lo_kinds = [
        (0, me.xo_z, me.zp), (1, me.xp_z, me.xp), (2, me.xm_z, me.xm),
        (3, me.xp, me.xp), (4, me.xm, me.xm), (5, me.xo, None), (6, me.zp, me.zp),
    ]

    def lo_piece(owner, k):
        return s.ls.at[owner, pl.ds(k * OG_ROWS, OG_ROWS)]

    def lo_slot(kind, k):
        return s.lo.at[kind, pl.ds(k * OG_ROWS, OG_ROWS)]

    def lo_start(kind, k):
        _, owner, to = lo_kinds[kind]
        if to is None:
            to = jnp.where(k % 2 == 0, me.xm, me.xp)
        send(lo_piece(owner, k), lo_slot(kind, k), s.lo_send.at[kind, k], s.lo_recv.at[kind, k], me.on_head(to))

    def lo_come(kind, k):
        arrived(lo_slot(kind, k), s.lo_recv.at[kind, k], me.on_head(me.zp))
        return lo_slot(kind, k)[...].astype(jnp.float32)

    def lo_add(owner, k, kinds):
        at = pl.ds(k * OG_ROWS, OG_ROWS)
        total = s.ls[owner, at].astype(jnp.float32)
        for kind in kinds:
            total = total + lo_come(kind, k)
        return total.astype(jnp.bfloat16)

    def share(owner, k):
        cols = pl.ds(pl.multiple_of(owner * NG * HD, NG * HD), NG * HD)
        rows = s.att[pl.ds(k * OG_ROWS, OG_ROWS)].reshape(OG_ROWS * BLK, NG * HD)
        out = dot(rows, s.weight[:, cols], 1, 0).astype(jnp.bfloat16)
        s.ls[owner, pl.ds(k * OG_ROWS, OG_ROWS)] = out.reshape(OG_ROWS, BLK, NG * HD)

    def shares(k):
        for kind in range(5):
            share(lo_kinds[kind][1], k)
            if kind < 3:
                lo_start(kind, k)
        even = k % 2 == 0

        @pl.when(even)
        def _():
            lo_start(3, k)

        @pl.when(jnp.logical_not(even))
        def _():
            lo_start(4, k)

        share(me.xo, k)
        share(me.zp, k)
        share(me.h, k)

    def lo_pass(k):
        at = pl.ds(k * OG_ROWS, OG_ROWS)
        s.ls[me.xo, at] = lo_add(me.xo, k, (0,))
        lo_start(5, k)
        s.ls[me.zp, at] = lo_add(me.zp, k, (1, 2))
        lo_start(6, k)

    def lo_last(k):
        at = pl.ds(k * OG_ROWS, OG_ROWS)
        even = k % 2 == 0
        owner = jnp.where(even, me.xm, me.xp)
        s.ls[owner, at] = lo_add(owner, k, (5,))

        @pl.when(even)
        def _():
            lo_start(4, k)

        @pl.when(jnp.logical_not(even))
        def _():
            lo_start(3, k)

    def lo_final(k):
        layer_out[pl.ds(k * OG_ROWS, OG_ROWS)] = lo_add(me.h, k, (3, 4, 6))

    forward_row(0, 2, index, q, s)
    kv_near(2)
    forward_row(1, 4, index, q, s)
    og_far(3)
    kv_far(1)
    og_near(1)
    shares(0)

    @pl.loop(1, KV_PARTS)
    def _(k):
        kv_ready(k)

        @pl.loop(0, 2)
        def _(half):
            @pl.when((half == 1) & (k == 1))
            def _():
                kv_near(3)
                og_near(0)

            @pl.when((half == 1) & (k < KV_PARTS - 1))
            def _():
                kv_far(k + 1)

            @pl.when(half == 1)
            def _():
                og_far(KV_PARTS - 1 - k)

            forward_row(2 * k + half, NCH, index, q, s)

        shares(k)

    def og_ready(k):
        for kind, owner in ((4, me.xm_z), (5, me.xp_z), (6, me.xo_z)):
            og_come(kind, owner, k)

    def project_grad(k):
        at = pl.ds(k * OG_ROWS, OG_ROWS)
        total = s.acc[at].reshape(OG_ROWS * BLK, NG * HD)
        for owner in (me.zp, me.xo, me.xm_z, me.xp_z, me.xo_z):
            cols = pl.ds(pl.multiple_of(owner * NG * HD, NG * HD), NG * HD)
            rows = s.og[owner, at].reshape(OG_ROWS * BLK, NG * HD)
            total = total + dot(rows, s.weight[:, cols], 1, 1)
        s.g[at] = total.astype(jnp.bfloat16).reshape(OG_ROWS, BLK, NG * HD)

    def kv_first(i):
        at = i % HELD

        @pl.when(i < ROWS - HELD)
        def _():
            sent(s.s1.at[at], s.send1.at[i + HELD], me.on_ctx(me.sib))

        collect_row(i, 1 - me.core, n_ctx, index, s, s.s1.at[at])
        send(s.s1.at[at], s.r1.at[i], s.send1.at[i], s.recv1.at[i], me.on_ctx(me.sib))
        collect_row(i, me.core, n_ctx, index, s, s.s2.at[i])

    def kv_second(i):
        arrived(s.r1.at[i], s.recv1.at[i], me.on_ctx(me.sib))
        s.s2[i] = (s.s2[i].astype(jnp.float32) + s.r1[i].astype(jnp.float32)).astype(jnp.bfloat16)
        for kind, to in enumerate((me.yp, me.ym)):
            src = s.s2.at[i, pl.ds(2 * me.ys[kind], 2)]
            send(src, s.r2.at[i, kind], s.send2.at[i, kind], s.recv2.at[i, kind], me.on_ctx(to))
        send(far_share(i, 1 - me.zh), s.r2.at[i, 2, 0], s.send4.at[i], s.recv4.at[i], me.on_ctx(me.zhp))

    def kv_direct():
        arrived(s.r1.at[0], s.recv1.at[0], me.on_ctx(me.sib))
        s.s2[0] = (s.s2[0].astype(jnp.float32) + s.r1[0].astype(jnp.float32)).astype(jnp.bfloat16)
        for k, to in enumerate(column):
            send(s.s2.at[0, to // 2], direct_slot(k), s.send5.at[k], s.recv5.at[k], me.on_ctx(to))

    def direct_slot(k):
        return s.r2.at[0, k // 2, k % 2] if k < 6 else s.r3.at[0]

    def kv_direct_final():
        total = s.s2[0, me.c // 2].astype(jnp.float32)
        for k in range(7):
            arrived(direct_slot(k), s.recv5.at[k], me.on_ctx(me.sib))
            total = total + direct_slot(k)[...].astype(jnp.float32)
        kv_write(0, total)

    def kv_write(i, total):
        dk[i] = (total[:, :HD] * SCALE).astype(jnp.bfloat16)
        dv[i] = total[:, HD:].astype(jnp.bfloat16)

    def far_share(i, zh):
        return s.s2.at[i, 2 * me.ys[2] + zh]

    def kv_far_sum(i):
        arrived(s.r2.at[i, 2, 0], s.recv4.at[i], me.on_ctx(me.zhp))
        ref = far_share(i, me.zh)
        ref[...] = (ref[...].astype(jnp.float32) + s.r2[i, 2, 0].astype(jnp.float32)).astype(jnp.bfloat16)
        send(ref, s.r2.at[i, 2, 1], s.send2.at[i, 2], s.recv2.at[i, 2], me.on_ctx(me.yo))

    def kv_sum(i, zh):
        total = s.s2[i, 2 * me.y + zh].astype(jnp.float32)
        for kind in range(2):
            total = total + s.r2[i, kind, zh].astype(jnp.float32)
        return total

    def kv_third(i):
        kv_far_sum(i)
        for kind in range(2):
            arrived(s.r2.at[i, kind], s.recv2.at[i, kind], me.on_ctx(me.sib))
        s.s3[i] = kv_sum(i, 1 - me.zh).astype(jnp.bfloat16)
        send(s.s3.at[i], s.r3.at[i], s.send3.at[i], s.recv3.at[i], me.on_ctx(me.zhp))

    def kv_final(i):
        arrived(s.r3.at[i], s.recv3.at[i], me.on_ctx(me.sib))
        arrived(s.r2.at[i, 2, 1], s.recv2.at[i, 2], me.on_ctx(me.sib))
        total = kv_sum(i, me.zh) + s.r3[i].astype(jnp.float32) + s.r2[i, 2, 1].astype(jnp.float32)
        kv_write(i, total)

    def step(n, count):
        i = ROWS - 1 - n
        backward_row(i, count, index, s)
        kv_first(i)

        @pl.when(n >= 1)
        def _():
            kv_second(i + 1)

        @pl.when(n >= 3)
        def _():
            kv_third(i + 3)

        @pl.when(n >= 5)
        def _():
            kv_final(i + 5)

    @pl.loop(0, ROWS - 2)
    def _(n):
        @pl.when(n % 2 == 0)
        def _():
            og_ready(OG_PARTS - 1 - n // 2)
            project_grad(OG_PARTS - 1 - n // 2)

        step(n, NCH)

        @pl.when((n >= 1) & (n < 1 + OG_PARTS))
        def _():
            lo_pass(n - 1)

        @pl.when(n >= 3)
        def _():
            lo_last(n - 3)

    og_ready(0)
    project_grad(0)
    step(ROWS - 2, 4)
    lo_last(3)
    step(ROWS - 1, 2)
    def query_rows(low):
        @pl.loop(low, low + 2)
        def _(i):
            query_row(i, NCH, index, s)

    query_rows(6)
    kv_direct()
    kv_third(2)
    query_rows(4)
    kv_third(1)
    lo_final(0)
    lo_final(1)
    query_rows(2)
    kv_final(4)
    kv_final(3)
    kv_final(1)
    kv_final(2)
    query_row(1, 4, index, s)
    query_row(0, 2, index, s)
    lo_final(2)
    lo_final(3)
    kv_direct_final()

    @pl.loop(0, OG_PARTS)
    def _(k):
        for kind, owner, to in og_kinds.values():
            og_gone(kind, owner, k)
        og_gone(2, me.xm, k)
        for kind, owner, to in lo_kinds:
            sent(lo_piece(owner, k), s.lo_send.at[kind, k], me.on_head(me.zp))

    @pl.loop(0, KV_PARTS)
    def _(k):
        for kind, owner, to in kv_kinds:
            kv_gone(kind, owner, k)

    for k in range(7):
        sent(s.s2.at[0, 0], s.send5.at[k], me.on_ctx(me.sib))

    @pl.loop(1, ROWS)
    def _(i):
        for kind in range(2):
            sent(s.s2.at[i, pl.ds(0, 2)], s.send2.at[i, kind], me.on_ctx(me.sib))
        sent(s.s2.at[i, 0], s.send2.at[i, 2], me.on_ctx(me.sib))
        sent(s.s2.at[i, 0], s.send4.at[i], me.on_ctx(me.sib))
        sent(s.s3.at[i], s.send3.at[i], me.on_ctx(me.zhp))

    @pl.loop(0, HELD)
    def _(i):
        sent(s.s1.at[i], s.send1.at[i], me.on_ctx(me.sib))


def hand_over_kernel(*refs):
    count = len(refs) // 2
    for k in range(count):
        refs[count + k][...] = refs[k][...]


def hand_over(arrays):
    vmem = pl.BlockSpec(memory_space=pltpu.VMEM)
    return pl.pallas_call(
        hand_over_kernel,
        out_shape=[jax.ShapeDtypeStruct(x.shape, x.dtype) for x in arrays],
        in_specs=[vmem] * len(arrays),
        out_specs=[vmem] * len(arrays),
        name="hand_over",
    )(*arrays)


def layer(index, q, key, value, out_grad, weight, n_head, n_ctx):
    smem = pl.BlockSpec(memory_space=pltpu.SMEM)
    vmem = pl.BlockSpec(memory_space=pltpu.VMEM)
    wide, narrow = (ROWS, BLK, NG * HD), (ROWS, BLK, HD)
    low = jnp.bfloat16
    sem = pltpu.SemaphoreType.DMA
    return pl.pallas_call(
        functools.partial(layer_kernel, n_ctx),
        out_shape=[jax.ShapeDtypeStruct(shape, low) for shape in (wide, wide, narrow, narrow)],
        in_specs=[smem] + [vmem] * 4 + [pl.BlockSpec(memory_space=pl.ANY)],
        out_specs=[vmem] * 4,
        scratch_shapes=[
            pltpu.VMEM((ROWS, QN, HD), low),
            pltpu.VMEM((NCH, CK, 2 * HD), low),
            pltpu.VMEM((NCH, CK, QN), jnp.float32),
            pltpu.VMEM((CHUNKS, CK, QN), low),
            pltpu.VMEM((ROWS, HD, QN), low),
            pltpu.VMEM((ROWS, 8, QN), jnp.float32),
            pltpu.VMEM((NOSLOT + 1, BLK, 2 * HD), low),
            pltpu.VMEM(wide, low),
            pltpu.VMEM(wide, low),
            pltpu.VMEM(wide, jnp.float32),
            pltpu.VMEM(weight.shape, low),
            pltpu.VMEM((n_ctx * ROWS, BLK, 2 * HD), low),
            pltpu.VMEM((n_ctx * ROWS, BLK, 2 * HD), low),
            pltpu.VMEM((n_head,) + wide, low),
            pltpu.VMEM((n_head,) + wide, low),
            pltpu.VMEM((7,) + wide, low),
            pltpu.VMEM((HELD, n_ctx // 2, BLK, 2 * HD), low),
            pltpu.VMEM((ROWS, n_ctx // 2, BLK, 2 * HD), low),
            pltpu.VMEM((ROWS, n_ctx // 2, BLK, 2 * HD), low),
            pltpu.VMEM((ROWS, 3, 2, BLK, 2 * HD), low),
            pltpu.VMEM((ROWS, BLK, 2 * HD), low),
            pltpu.VMEM((ROWS, BLK, 2 * HD), low),
            sem,
            sem((7, OG_PARTS)), sem((7, OG_PARTS)),
            sem((15, KV_PARTS)), sem((15, KV_PARTS)),
            sem((7, OG_PARTS)), sem((7, OG_PARTS)),
            sem((ROWS,)), sem((ROWS,)),
            sem((ROWS, 3)), sem((ROWS, 3)),
            sem((ROWS,)), sem((ROWS,)),
            sem((ROWS,)), sem((ROWS,)),
            sem((7,)), sem((7,)),
        ],
        compiler_params=pltpu.CompilerParams(
            vmem_limit_bytes=63 << 20, collective_id=0, has_side_effects=True
        ),
        name="layer",
    )(index, q, key, value, out_grad, weight)


def on_device(query, key, value, out_grad, weight, vertical, slash):
    n_head, n_ctx = lax.axis_size("head"), lax.axis_size("ctx")
    index = lists(vertical[0, :, 0], slash[0, :, 0], lax.axis_index("ctx"), n_ctx)
    outs = layer(
        index, query[:, 0], key[:, 0], value[:, 0], out_grad[:, 0], weight, n_head, n_ctx
    )
    return tuple(x[:, None] for x in hand_over(outs))


def solution(mesh):
    spread = P(None, "ctx", None, "head")
    listed = P("head", None, "ctx", None)
    return jax.shard_map(
        on_device,
        mesh=mesh,
        in_specs=(spread, spread, spread, spread, P("head", None), listed, listed),
        out_specs=(spread,) * 4,
        check_vma=False,
    )
```

```python
import functools
import math

import jax
import jax.numpy as jnp
from jax import lax
from jax.experimental import pallas as pl
from jax.experimental.pallas import tpu as pltpu
from jax.sharding import PartitionSpec as P

HD = 128
NG = 4
BLK = 64
ROWS = 8
NE = 40
EPC = 8
CK = EPC * BLK
NCH = NE // EPC
QN = NG * BLK
CHUNKS = 36
NOSLOT = 0
FIRST = 1
SCALE = 1.0 / math.sqrt(HD)
LOG2E = 1.4426950408889634
FAR = -1e30


def chunk_base(i):
    return jnp.where(i == 0, 0, jnp.where(i == 1, 2, 5 * i - 4))


def lists(vertical, slash, me, n_ctx):
    rows = jnp.arange(ROWS, dtype=jnp.int32)
    bid = rows * n_ctx + me
    raw = jnp.concatenate([bid[:, None] - slash, vertical], axis=1)
    kept = (raw >= 0) & (raw <= bid[:, None])
    order = jnp.arange(NE, dtype=jnp.int32)
    place = jnp.sum((kept[:, None, :] & (order[None, None, :] < order[None, :, None])).astype(jnp.int32), axis=2)
    place = jnp.where(kept, place, NE)
    moved = raw % n_ctx * ROWS + raw // n_ctx
    slot = FIRST + chunk_base(rows)[:, None] * EPC + place
    blocks = ROWS * n_ctx
    column = jnp.arange(NE + blocks + 1, dtype=jnp.int32)[None, :, None]
    by_place = place[:, None, :] == column
    by_block = kept[:, None, :] & (raw[:, None, :] == column - NE)
    last = column == NE + blocks
    picked = jnp.where(by_place & (column < NE), moved[:, None, :], 0)
    picked = jnp.where(by_block, slot[:, None, :], picked)
    picked = jnp.where(last, kept[:, None, :].astype(jnp.int32), picked)
    return jnp.sum(picked, axis=2)


def dot(a, b, ca, cb):
    return lax.dot_general(a, b, (((ca,), (cb,)), ((), ())), preferred_element_type=jnp.float32)


def heads_down(x):
    return jnp.concatenate([x[:, h * HD:(h + 1) * HD] for h in range(NG)], axis=0)


def heads_across(x):
    return jnp.concatenate([x[h * BLK:(h + 1) * BLK] for h in range(NG)], axis=1)


def forward_row(i, count, index, q, s):
    qs = heads_down(q[i])
    s.qs[i] = qs
    base = chunk_base(i)
    key_pos = lax.broadcasted_iota(jnp.int32, (BLK, QN), 0)
    query_pos = lax.broadcasted_iota(jnp.int32, (BLK, QN), 1) % BLK
    top = jnp.full((8, QN), FAR, jnp.float32)
    entries = index[i, index.shape[1] - 1]

    def far(at):
        return jnp.where(at < entries, 0.0, FAR)

    for ch in range(count):
        for e in range(EPC):
            s.kvrow[ch, e * BLK:(e + 1) * BLK, :] = s.table[index[i, ch * EPC + e]]
        sc = dot(s.kvrow[ch, :, :HD], qs, 1, 1)
        for e in range(EPC):
            part = sc[e * BLK:(e + 1) * BLK]
            if ch == 0 and e == 0:
                part = jnp.where(key_pos <= query_pos, part, FAR)
            s.sc[ch, e * BLK:(e + 1) * BLK, :] = part
            part = jnp.max(part.reshape(BLK // 8, 8, QN), axis=0)
            top = jnp.maximum(top, part + far(ch * EPC + e))
    top = jnp.max(top, axis=0, keepdims=True) * (SCALE * LOG2E)

    total = jnp.zeros((8, QN), jnp.float32)
    acc = jnp.zeros((HD, QN), jnp.float32)
    for ch in range(count):
        for e in range(EPC):
            shift = top - far(ch * EPC + e)
            p = jnp.exp2(s.sc[ch, e * BLK:(e + 1) * BLK, :] * (SCALE * LOG2E) - shift)
            total = total + jnp.sum(p.reshape(BLK // 8, 8, QN), axis=0)
            s.p[base + ch, e * BLK:(e + 1) * BLK, :] = p.astype(jnp.bfloat16)
        acc = acc + dot(s.kvrow[ch, :, HD:], s.p[base + ch], 0, 0)
    inv = 1.0 / jnp.sum(total, axis=0, keepdims=True)
    out = (acc * inv).astype(jnp.bfloat16)
    s.ot[i] = out
    s.inv[i] = jnp.broadcast_to(inv, (8, QN))
    s.att[i] = heads_across(out.astype(jnp.float32).T.astype(jnp.bfloat16))


def backward_row(i, count, index, s):
    base = chunk_base(i)
    gt = heads_down(s.g[i].astype(jnp.float32)).T
    gt = (gt * s.inv[i][0:1]).astype(jnp.bfloat16)
    g32 = gt.astype(jnp.float32)
    delta = jnp.sum(g32 * s.ot[i].astype(jnp.float32), axis=0, keepdims=True)
    gs = g32.T.astype(jnp.bfloat16)
    qs = s.qs[i]
    for ch in range(count):
        for e in range(EPC):
            s.kvrow[ch, e * BLK:(e + 1) * BLK, HD:] = s.table[index[i, ch * EPC + e], :, HD:]
        dp = dot(s.kvrow[ch, :, HD:], gt, 1, 0)
        p = s.p[base + ch]
        ds = (p.astype(jnp.float32) * (dp - delta)).astype(jnp.bfloat16)
        at = pl.ds(FIRST + (base + ch) * EPC, EPC)
        s.slots[at, :, :HD] = dot(ds, qs, 1, 0).astype(jnp.bfloat16).reshape(EPC, BLK, HD)
        s.slots[at, :, HD:] = dot(p, gs, 1, 0).astype(jnp.bfloat16).reshape(EPC, BLK, HD)
        s.p[base + ch] = ds


def query_row(i, count, index, s):
    acc = jnp.zeros((HD, QN), jnp.float32)
    base = chunk_base(i)
    for ch in range(count):
        for e in range(EPC):
            s.kvrow[ch, e * BLK:(e + 1) * BLK, :HD] = s.table[index[i, ch * EPC + e], :, :HD]
        acc = acc + dot(s.kvrow[ch, :, :HD], s.p[base + ch], 0, 0)
    s.dq[i] = heads_across((acc * SCALE).T).astype(jnp.bfloat16)


def collect(first, u, index, s):
    total = s.slots[index[first, NE + u]].astype(jnp.float32)
    for r in range(first + 1, ROWS):
        total = total + s.slots[index[r, NE + u]].astype(jnp.float32)
    return total


def collect_row(i, core, n_ctx, index, s, out):
    for first in range(ROWS):

        @pl.when(i == first)
        def _():
            @pl.loop(0, n_ctx // 2)
            def _(j):
                out[j] = collect(first, first * n_ctx + 2 * j + core, index, s).astype(jnp.bfloat16)


class Scratch:
    pass


MESH = pl.DeviceIdType.MESH
OG_PARTS = 4
OG_ROWS = ROWS // OG_PARTS
HELD = 4
KV_PARTS = 4
OVER_Y = 2
KV_ROWS = ROWS // KV_PARTS


def send(src, dst, send_sem, recv_sem, device):
    pltpu.make_async_remote_copy(
        src_ref=src, dst_ref=dst, send_sem=send_sem, recv_sem=recv_sem, device_id=device, device_id_type=MESH
    ).start()


def sent(src, sem, device):
    pltpu.make_async_remote_copy(
        src_ref=src, dst_ref=src, send_sem=sem, recv_sem=sem, device_id=device, device_id_type=MESH
    ).wait_send()


def arrived(dst, sem, device):
    pltpu.make_async_remote_copy(
        src_ref=dst, dst_ref=dst, send_sem=sem, recv_sem=sem, device_id=device, device_id_type=MESH
    ).wait_recv()


class Place:
    def __init__(self):
        h, c = lax.axis_index("head"), lax.axis_index("ctx")
        self.h, self.c = h, c
        x, zl = h // 2, h % 2
        y, zh, core = c // 4, c // 2 % 2, c % 2
        self.y, self.zh, self.core = y, zh, core
        self.xp, self.xm, self.xo = [(x + k) % 4 * 2 + zl for k in (1, 3, 2)]
        self.zp = x * 2 + 1 - zl
        flip = 1 - 2 * zl
        self.xp_z, self.xm_z, self.xo_z = self.xp + flip, self.xm + flip, self.xo + flip
        self.ys = [(y + k) % 4 for k in (1, 3, 2)]
        self.yp, self.ym, self.yo = [v * 4 + zh * 2 + core for v in self.ys]
        turn = 2 * (1 - 2 * zh)
        self.zhp = c + turn
        self.yp_z, self.ym_z, self.yo_z = self.yp + turn, self.ym + turn, self.yo + turn
        self.other = 1 - 2 * core
        self.sib = c + self.other

    def on_head(self, index):
        return (index, self.c)

    def on_ctx(self, index):
        return (self.h, index)


def gather_out_grad(me, s):
    def piece(owner, k):
        return s.og.at[owner, pl.ds(k * OG_ROWS, OG_ROWS)]

    def go(kind, owner, to, k):
        ref = piece(owner, k)
        send(ref, ref, s.og_send.at[kind, k], s.og_recv.at[kind, k], me.on_head(to))

    def come(kind, owner, k):
        arrived(piece(owner, k), s.og_recv.at[kind, k], me.on_head(me.zp))

    def gone(kind, owner, k):
        sent(piece(owner, k), s.og_send.at[kind, k], me.on_head(me.zp))

    return go, come, gone


def gather_kv(me, s):
    def piece(owner, k):
        return s.kv.at[pl.ds(owner * ROWS + k * KV_ROWS, KV_ROWS)]

    def go(kind, owner, to, k):
        ref = piece(owner, k)
        send(ref, ref, s.kv_send.at[kind, k], s.kv_recv.at[kind, k], me.on_ctx(to))

    def come(kind, owner, k):
        arrived(piece(owner, k), s.kv_recv.at[kind, k], me.on_ctx(me.sib))

    def gone(kind, owner, k):
        sent(piece(owner, k), s.kv_send.at[kind, k], me.on_ctx(me.sib))

    return go, come, gone


def layer_kernel(n_ctx, index, query, key, value, out_grad, weight, layer_out, dq, dk, dv, *refs):
    s = Scratch()
    (
        s.qs, s.kvrow, s.sc, s.p, s.ot, s.inv, s.slots, s.att, s.g, s.acc, s.q, s.weight, s.kv, s.table, s.og,
        s.ls, s.lo, s.s1, s.r1, s.s2, s.r2, s.s3, s.r3, w_sem, q_sem,
        s.og_send, s.og_recv, s.kv_send, s.kv_recv, s.lo_send, s.lo_recv,
        s.send1, s.recv1, s.send2, s.recv2, s.send3, s.recv3, s.send4, s.recv4, s.send5, s.recv5,
    ) = refs
    s.dq = dq
    me = Place()
    w_copy = pltpu.make_async_copy(weight, s.weight, w_sem)
    w_copy.start()
    q_copy = pltpu.make_async_copy(query, s.q, q_sem)
    q_copy.start()
    mine = pl.multiple_of(me.c * ROWS, ROWS)
    s.kv[pl.ds(mine, ROWS), :, :HD] = key[...]
    s.kv[pl.ds(mine, ROWS), :, HD:] = value[...]
    s.og[me.h] = out_grad[...]

    barrier = pltpu.get_barrier_semaphore()
    partners = [me.on_head(d) for d in (me.xp, me.xm, me.xo, me.zp)]
    column = (me.yp, me.ym, me.yo, me.yp_z, me.ym_z, me.yo_z, me.zhp)
    partners += [me.on_ctx(d) for d in column + (me.sib,)]
    for device in partners:
        pl.semaphore_signal(barrier, inc=1, device_id=device, device_id_type=MESH)
    pl.semaphore_wait(barrier, len(partners))

    og_go, og_come, og_gone = gather_out_grad(me, s)
    kv_go, kv_come, kv_gone = gather_kv(me, s)
    kv_kinds = [
        (0, me.c, me.yp), (1, me.c, me.ym), (2, me.c, me.yo), (3, me.c, me.zhp),
        (4, me.zhp, me.yp), (5, me.zhp, me.ym), (6, me.zhp, me.yo),
        (7, me.c, me.sib), (8, me.zhp, me.sib), (9, me.ym, me.sib), (10, me.yp, me.sib), (11, me.yo, me.sib),
        (12, me.ym_z, me.sib), (13, me.yp_z, me.sib), (14, me.yo_z, me.sib),
    ]
    og_kinds = {
        0: (0, me.h, me.xp), 1: (1, me.h, me.xm), 3: (3, me.h, me.zp),
        4: (4, me.zp, me.xp), 5: (5, me.zp, me.xm), 6: (6, me.xo, me.zp),
    }

    def kv_start(kinds, k):
        for kind in kinds:
            kv_go(*kv_kinds[kind], k)

    def og_start(kinds, k):
        for kind in kinds:
            og_go(*og_kinds[kind], k)

    def og_across(k):
        og_come(0, me.xm, k)
        og_come(1, me.xp, k)
        og_go(2, me.xm if k % 2 == 0 else me.xp, me.xp if k % 2 == 0 else me.xm, k)

    def og_near(k):
        og_come(3, me.zp, k)
        og_start((4, 5), k)

    def og_far(k):
        og_come(2, me.xo, k)
        og_start((6,), k)

    def project_early(owner, first):
        cols = pl.ds(pl.multiple_of(owner * NG * HD, NG * HD), NG * HD)
        part = dot(s.og[owner].reshape(ROWS * BLK, NG * HD), s.weight[:, cols], 1, 1)
        part = part.reshape(ROWS, BLK, NG * HD)
        s.acc[...] = part if first else s.acc[...] + part

    def kv_pass(k):
        kv_come(3, me.zhp, k)
        if k < OVER_Y:
            kv_start((6,), k)
        kv_start((4, 5, 8), k)

    def kv_near(k):
        for kind, owner in ((0, me.ym), (1, me.yp), (2, me.yo)):
            kv_come(kind, owner, k)
        if k >= OVER_Y:
            kv_go(6, me.yo, me.zhp, k)
        kv_start((9, 10, 11), k)

    def kv_far(k):
        for kind, owner in ((4, me.ym_z), (5, me.yp_z), (6, me.yo_z)):
            kv_come(kind, owner, k)
        kv_start((12, 13, 14), k)

    def kv_ready(k):
        owners = (me.c, me.zhp, me.ym, me.yp, me.yo, me.ym_z, me.yp_z, me.yo_z)
        for kind, owner in enumerate(owners, 7):
            kv_come(kind, owner + me.other, k)

        @pl.loop(0, n_ctx)
        def _(c):
            at = pl.ds(c * ROWS + k * KV_ROWS, KV_ROWS)
            s.table[at] = s.kv[at]

    for k in range(KV_PARTS):
        kv_start((3,), k)
    for k in range(2):
        kv_start((2, 0, 1, 7), k)
        og_start((0, 1), OG_PARTS - 1 - k)
    og_start((3,), 3)
    og_start((3,), 2)
    og_start((0, 1), 1)
    og_start((0, 1), 0)
    s.slots[NOSLOT] = jnp.zeros((BLK, 2 * HD), jnp.bfloat16)
    kv_pass(0)
    kv_start((2, 0, 1, 7), 2)
    og_across(3)
    kv_pass(1)
    kv_start((2, 0, 1, 7), 3)
    kv_near(0)
    kv_pass(2)
    og_across(2)
    kv_pass(3)
    og_start((3,), 1)
    og_start((3,), 0)
    kv_near(1)
    og_across(1)
    og_near(3)
    kv_far(0)
    og_across(0)
    og_near(2)
    w_copy.wait()
    q_copy.wait()
    for owner in (me.h, me.xm, me.xp):
        project_early(owner, owner is me.h)
    kv_ready(0)

    lo_kinds = [
        (0, me.xo_z, me.zp), (1, me.xp_z, me.xp), (2, me.xm_z, me.xm),
        (3, me.xp, me.xp), (4, me.xm, me.xm), (5, me.xo, None), (6, me.zp, me.zp),
    ]

    def lo_piece(owner, k):
        return s.ls.at[owner, pl.ds(k * OG_ROWS, OG_ROWS)]

    def lo_slot(kind, k):
        return s.lo.at[kind, pl.ds(k * OG_ROWS, OG_ROWS)]

    def lo_start(kind, k):
        _, owner, to = lo_kinds[kind]
        if to is None:
            to = jnp.where(k % 2 == 0, me.xm, me.xp)
        send(lo_piece(owner, k), lo_slot(kind, k), s.lo_send.at[kind, k], s.lo_recv.at[kind, k], me.on_head(to))

    def lo_come(kind, k):
        arrived(lo_slot(kind, k), s.lo_recv.at[kind, k], me.on_head(me.zp))
        return lo_slot(kind, k)[...].astype(jnp.float32)

    def lo_add(owner, k, kinds):
        at = pl.ds(k * OG_ROWS, OG_ROWS)
        total = s.ls[owner, at].astype(jnp.float32)
        for kind in kinds:
            total = total + lo_come(kind, k)
        return total.astype(jnp.bfloat16)

    def share(owner, k):
        cols = pl.ds(pl.multiple_of(owner * NG * HD, NG * HD), NG * HD)
        rows = s.att[pl.ds(k * OG_ROWS, OG_ROWS)].reshape(OG_ROWS * BLK, NG * HD)
        out = dot(rows, s.weight[:, cols], 1, 0).astype(jnp.bfloat16)
        s.ls[owner, pl.ds(k * OG_ROWS, OG_ROWS)] = out.reshape(OG_ROWS, BLK, NG * HD)

    def shares(k):
        for kind in range(5):
            share(lo_kinds[kind][1], k)
            if kind < 3:
                lo_start(kind, k)
        even = k % 2 == 0

        @pl.when(even)
        def _():
            lo_start(3, k)

        @pl.when(jnp.logical_not(even))
        def _():
            lo_start(4, k)

        share(me.xo, k)
        share(me.zp, k)
        share(me.h, k)

    def lo_pass(k):
        at = pl.ds(k * OG_ROWS, OG_ROWS)
        s.ls[me.xo, at] = lo_add(me.xo, k, (0,))
        lo_start(5, k)
        s.ls[me.zp, at] = lo_add(me.zp, k, (1, 2))
        lo_start(6, k)

    def lo_last(k):
        at = pl.ds(k * OG_ROWS, OG_ROWS)
        even = k % 2 == 0
        owner = jnp.where(even, me.xm, me.xp)
        s.ls[owner, at] = lo_add(owner, k, (5,))

        @pl.when(even)
        def _():
            lo_start(4, k)

        @pl.when(jnp.logical_not(even))
        def _():
            lo_start(3, k)

    def lo_final(k):
        layer_out[pl.ds(k * OG_ROWS, OG_ROWS)] = lo_add(me.h, k, (3, 4, 6))

    forward_row(0, 2, index, s.q, s)
    kv_near(2)
    forward_row(1, 4, index, s.q, s)
    og_far(3)
    kv_far(1)
    og_near(1)
    shares(0)

    @pl.loop(1, KV_PARTS)
    def _(k):
        kv_ready(k)

        @pl.loop(0, 2)
        def _(half):
            @pl.when((half == 1) & (k == 1))
            def _():
                kv_near(3)
                og_near(0)

            @pl.when((half == 1) & (k < KV_PARTS - 1))
            def _():
                kv_far(k + 1)

            @pl.when(half == 1)
            def _():
                og_far(KV_PARTS - 1 - k)

            forward_row(2 * k + half, NCH, index, s.q, s)

        shares(k)

    def og_ready(k):
        for kind, owner in ((4, me.xm_z), (5, me.xp_z), (6, me.xo_z)):
            og_come(kind, owner, k)

    def project_grad(k):
        at = pl.ds(k * OG_ROWS, OG_ROWS)
        total = s.acc[at].reshape(OG_ROWS * BLK, NG * HD)
        for owner in (me.zp, me.xo, me.xm_z, me.xp_z, me.xo_z):
            cols = pl.ds(pl.multiple_of(owner * NG * HD, NG * HD), NG * HD)
            rows = s.og[owner, at].reshape(OG_ROWS * BLK, NG * HD)
            total = total + dot(rows, s.weight[:, cols], 1, 1)
        s.g[at] = total.astype(jnp.bfloat16).reshape(OG_ROWS, BLK, NG * HD)

    def kv_first(i):
        at = i % HELD

        @pl.when(i < ROWS - HELD)
        def _():
            sent(s.s1.at[at], s.send1.at[i + HELD], me.on_ctx(me.sib))

        collect_row(i, 1 - me.core, n_ctx, index, s, s.s1.at[at])
        send(s.s1.at[at], s.r1.at[i], s.send1.at[i], s.recv1.at[i], me.on_ctx(me.sib))
        collect_row(i, me.core, n_ctx, index, s, s.s2.at[i])

    def kv_second(i):
        arrived(s.r1.at[i], s.recv1.at[i], me.on_ctx(me.sib))
        s.s2[i] = (s.s2[i].astype(jnp.float32) + s.r1[i].astype(jnp.float32)).astype(jnp.bfloat16)
        for kind, to in enumerate((me.yp, me.ym)):
            src = s.s2.at[i, pl.ds(2 * me.ys[kind], 2)]
            send(src, s.r2.at[i, kind], s.send2.at[i, kind], s.recv2.at[i, kind], me.on_ctx(to))
        send(far_share(i, 1 - me.zh), s.r2.at[i, 2, 0], s.send4.at[i], s.recv4.at[i], me.on_ctx(me.zhp))

    def kv_direct():
        arrived(s.r1.at[0], s.recv1.at[0], me.on_ctx(me.sib))
        s.s2[0] = (s.s2[0].astype(jnp.float32) + s.r1[0].astype(jnp.float32)).astype(jnp.bfloat16)
        for k, to in enumerate(column):
            send(s.s2.at[0, to // 2], direct_slot(k), s.send5.at[k], s.recv5.at[k], me.on_ctx(to))

    def direct_slot(k):
        return s.r2.at[0, k // 2, k % 2] if k < 6 else s.r3.at[0]

    def kv_direct_final():
        total = s.s2[0, me.c // 2].astype(jnp.float32)
        for k in range(7):
            arrived(direct_slot(k), s.recv5.at[k], me.on_ctx(me.sib))
            total = total + direct_slot(k)[...].astype(jnp.float32)
        kv_write(0, total)

    def kv_write(i, total):
        dk[i] = (total[:, :HD] * SCALE).astype(jnp.bfloat16)
        dv[i] = total[:, HD:].astype(jnp.bfloat16)

    def far_share(i, zh):
        return s.s2.at[i, 2 * me.ys[2] + zh]

    def kv_far_sum(i):
        arrived(s.r2.at[i, 2, 0], s.recv4.at[i], me.on_ctx(me.zhp))
        ref = far_share(i, me.zh)
        ref[...] = (ref[...].astype(jnp.float32) + s.r2[i, 2, 0].astype(jnp.float32)).astype(jnp.bfloat16)
        send(ref, s.r2.at[i, 2, 1], s.send2.at[i, 2], s.recv2.at[i, 2], me.on_ctx(me.yo))

    def kv_sum(i, zh):
        total = s.s2[i, 2 * me.y + zh].astype(jnp.float32)
        for kind in range(2):
            total = total + s.r2[i, kind, zh].astype(jnp.float32)
        return total

    def kv_third(i):
        kv_far_sum(i)
        for kind in range(2):
            arrived(s.r2.at[i, kind], s.recv2.at[i, kind], me.on_ctx(me.sib))
        s.s3[i] = kv_sum(i, 1 - me.zh).astype(jnp.bfloat16)
        send(s.s3.at[i], s.r3.at[i], s.send3.at[i], s.recv3.at[i], me.on_ctx(me.zhp))

    def kv_final(i):
        arrived(s.r3.at[i], s.recv3.at[i], me.on_ctx(me.sib))
        arrived(s.r2.at[i, 2, 1], s.recv2.at[i, 2], me.on_ctx(me.sib))
        total = kv_sum(i, me.zh) + s.r3[i].astype(jnp.float32) + s.r2[i, 2, 1].astype(jnp.float32)
        kv_write(i, total)

    def step(n, count):
        i = ROWS - 1 - n
        backward_row(i, count, index, s)
        kv_first(i)

        @pl.when(n >= 1)
        def _():
            kv_second(i + 1)

        @pl.when(n >= 3)
        def _():
            kv_third(i + 3)

        @pl.when(n >= 5)
        def _():
            kv_final(i + 5)

    @pl.loop(0, ROWS - 2)
    def _(n):
        @pl.when(n % 2 == 0)
        def _():
            og_ready(OG_PARTS - 1 - n // 2)
            project_grad(OG_PARTS - 1 - n // 2)

        step(n, NCH)

        @pl.when((n >= 1) & (n < 1 + OG_PARTS))
        def _():
            lo_pass(n - 1)

        @pl.when(n >= 3)
        def _():
            lo_last(n - 3)

    og_ready(0)
    project_grad(0)
    step(ROWS - 2, 4)
    lo_last(3)
    step(ROWS - 1, 2)
    def query_rows(low):
        @pl.loop(low, low + 2)
        def _(i):
            query_row(i, NCH, index, s)

    query_rows(6)
    kv_direct()
    kv_third(2)
    query_rows(4)
    kv_third(1)
    lo_final(0)
    lo_final(1)
    query_rows(2)
    kv_final(4)
    kv_final(3)
    kv_final(1)
    kv_final(2)
    query_row(1, 4, index, s)
    query_row(0, 2, index, s)
    lo_final(2)
    lo_final(3)
    kv_direct_final()

    @pl.loop(0, OG_PARTS)
    def _(k):
        for kind, owner, to in og_kinds.values():
            og_gone(kind, owner, k)
        og_gone(2, me.xm, k)
        for kind, owner, to in lo_kinds:
            sent(lo_piece(owner, k), s.lo_send.at[kind, k], me.on_head(me.zp))

    @pl.loop(0, KV_PARTS)
    def _(k):
        for kind, owner, to in kv_kinds:
            kv_gone(kind, owner, k)

    for k in range(7):
        sent(s.s2.at[0, 0], s.send5.at[k], me.on_ctx(me.sib))

    @pl.loop(1, ROWS)
    def _(i):
        for kind in range(2):
            sent(s.s2.at[i, pl.ds(0, 2)], s.send2.at[i, kind], me.on_ctx(me.sib))
        sent(s.s2.at[i, 0], s.send2.at[i, 2], me.on_ctx(me.sib))
        sent(s.s2.at[i, 0], s.send4.at[i], me.on_ctx(me.sib))
        sent(s.s3.at[i], s.send3.at[i], me.on_ctx(me.zhp))

    @pl.loop(0, HELD)
    def _(i):
        sent(s.s1.at[i], s.send1.at[i], me.on_ctx(me.sib))


def hand_over_kernel(*refs):
    count = len(refs) // 2
    for k in range(count):
        refs[count + k][...] = refs[k][...]


def hand_over(arrays):
    vmem = pl.BlockSpec(memory_space=pltpu.VMEM)
    return pl.pallas_call(
        hand_over_kernel,
        out_shape=[jax.ShapeDtypeStruct(x.shape, x.dtype) for x in arrays],
        in_specs=[vmem] * len(arrays),
        out_specs=[vmem] * len(arrays),
        name="hand_over",
    )(*arrays)


def layer(index, q, key, value, out_grad, weight, n_head, n_ctx):
    smem = pl.BlockSpec(memory_space=pltpu.SMEM)
    vmem = pl.BlockSpec(memory_space=pltpu.VMEM)
    wide, narrow = (ROWS, BLK, NG * HD), (ROWS, BLK, HD)
    low = jnp.bfloat16
    sem = pltpu.SemaphoreType.DMA
    return pl.pallas_call(
        functools.partial(layer_kernel, n_ctx),
        out_shape=[jax.ShapeDtypeStruct(shape, low) for shape in (wide, wide, narrow, narrow)],
        in_specs=[smem, pl.BlockSpec(memory_space=pl.ANY)] + [vmem] * 3 + [pl.BlockSpec(memory_space=pl.ANY)],
        out_specs=[vmem] * 4,
        scratch_shapes=[
            pltpu.VMEM((ROWS, QN, HD), low),
            pltpu.VMEM((NCH, CK, 2 * HD), low),
            pltpu.VMEM((NCH, CK, QN), jnp.float32),
            pltpu.VMEM((CHUNKS, CK, QN), low),
            pltpu.VMEM((ROWS, HD, QN), low),
            pltpu.VMEM((ROWS, 8, QN), jnp.float32),
            pltpu.VMEM((FIRST + CHUNKS * EPC, BLK, 2 * HD), low),
            pltpu.VMEM(wide, low),
            pltpu.VMEM(wide, low),
            pltpu.VMEM(wide, jnp.float32),
            pltpu.VMEM(wide, low),
            pltpu.VMEM(weight.shape, low),
            pltpu.VMEM((n_ctx * ROWS, BLK, 2 * HD), low),
            pltpu.VMEM((n_ctx * ROWS, BLK, 2 * HD), low),
            pltpu.VMEM((n_head,) + wide, low),
            pltpu.VMEM((n_head,) + wide, low),
            pltpu.VMEM((7,) + wide, low),
            pltpu.VMEM((HELD, n_ctx // 2, BLK, 2 * HD), low),
            pltpu.VMEM((ROWS, n_ctx // 2, BLK, 2 * HD), low),
            pltpu.VMEM((ROWS, n_ctx // 2, BLK, 2 * HD), low),
            pltpu.VMEM((ROWS, 3, 2, BLK, 2 * HD), low),
            pltpu.VMEM((ROWS, BLK, 2 * HD), low),
            pltpu.VMEM((ROWS, BLK, 2 * HD), low),
            sem,
            sem,
            sem((7, OG_PARTS)), sem((7, OG_PARTS)),
            sem((15, KV_PARTS)), sem((15, KV_PARTS)),
            sem((7, OG_PARTS)), sem((7, OG_PARTS)),
            sem((ROWS,)), sem((ROWS,)),
            sem((ROWS, 3)), sem((ROWS, 3)),
            sem((ROWS,)), sem((ROWS,)),
            sem((ROWS,)), sem((ROWS,)),
            sem((7,)), sem((7,)),
        ],
        compiler_params=pltpu.CompilerParams(
            vmem_limit_bytes=63 << 20, collective_id=0, has_side_effects=True
        ),
        name="layer",
    )(index, q, key, value, out_grad, weight)


def on_device(query, key, value, out_grad, weight, vertical, slash):
    n_head, n_ctx = lax.axis_size("head"), lax.axis_size("ctx")
    index = lists(vertical[0, :, 0], slash[0, :, 0], lax.axis_index("ctx"), n_ctx)
    outs = layer(
        index, query[:, 0], key[:, 0], value[:, 0], out_grad[:, 0], weight, n_head, n_ctx
    )
    return tuple(x[:, None] for x in hand_over(outs))


def solution(mesh):
    spread = P(None, "ctx", None, "head")
    listed = P("head", None, "ctx", None)
    return jax.shard_map(
        on_device,
        mesh=mesh,
        in_specs=(spread, spread, spread, spread, P("head", None), listed, listed),
        out_specs=(spread,) * 4,
        check_vma=False,
    )
```
